32 devices in a mesh: patch: 8 (over z, y), band: 4 (over x, core).
Axes of the slice: x: 2, y: 2, z: 4, core: 2. Of those that a mesh axis runs over, the one named last changes fastest.
Arguments:
- blocks: bfloat16 [4, 256, 256, 256], P('band', 'patch'), may hold values from -6 to 6
- dest_patch: int32 [4, 256], P('band', 'patch'), may hold values from 0 to 7, as said below
- dest_slot: int32 [4, 256], P('band', 'patch'), may hold values from 0 to 3
- weights: bfloat16 [4, 256], P('band', 'patch'), may hold values from 0.25 to 4
- psf_taps: bfloat16 [4, 256, 2, 41], P('band', 'patch'), may hold values from -1 to 1
- det_taps: float32 [4, 25], P('band'), may hold values from -1.25 to 1.25
- noise_var: float32 [4], P('band'), may hold values from 0.5 to 2
Outputs:
- coadd_image: float32 [4, 512, 4096], P('band', None, 'patch')
- chi_square: float32 [512, 4096], P('band', 'patch')
The draws below stay inside these ranges and needn't reach their ends.
Inputs may be any that keep to these rules, and one draw needn't show every extreme that they name: `dest_patch`: within each band, among the 32 blocks of one index of patch (aligned runs of 32 blocks), at most 4 go to any one patch; in every band some patch receives exactly 4 blocks from every index of patch.
All inputs are finite; a program needn't handle non-finite values.
Results may differ from the reference program's by a relative error of at most 0.0048.
Values may be sent and summed in bfloat16 or wider, within the bound.
No kernel may reach another device: no remote copies, remote signals or barrier semaphores. Data moves between devices by JAX's collectives and lax.ppermute only.
A program may use at most 192 MiB of HBM per device.

```python
import math
import jax
import jax.numpy as jnp
from jax import lax

BLK = 256
TH = 2
TW = 2
VB_DEV = 32
TAPS = 41
DR = 12
CAP = 4
DTAPS = 25
BANDS = 4
VISIT_BLOCKS = 256
SLOTS = 4
PH = 512
WIDTH = 4096


def draw_dest_patch(key, part):
    npatch = VISIT_BLOCKS // VB_DEV
    key_busy, key_perm, key_order = jax.random.split(jax.random.fold_in(key, 17), 3)
    busiest = jax.random.randint(key_busy, (BANDS, 1, 1), 0, npatch).astype(jnp.int32)
    scores = jax.random.randint(key_perm, (BANDS, npatch, npatch - 1), 0, 1 << 20) * (npatch - 1) + jnp.arange(npatch - 1, dtype=jnp.int32)
    others = jnp.argsort(scores, axis=-1, stable=True).astype(jnp.int32)
    places = jnp.arange(VB_DEV, dtype=jnp.int32)
    picked = jnp.maximum(places - CAP, 0) // CAP
    chosen = jnp.take(others, picked, axis=-1)
    chosen = chosen + (chosen >= busiest).astype(jnp.int32)
    target = jnp.where(places[None, None, :] < CAP, busiest, chosen)
    order_scores = jax.random.randint(key_order, (BANDS, npatch, VB_DEV), 0, 1 << 20) * VB_DEV + places
    ordering = jnp.argsort(order_scores, axis=-1, stable=True)
    target = jnp.take_along_axis(target, ordering, axis=-1)
    return target.reshape(BANDS, VISIT_BLOCKS).astype(jnp.int32)


def touch_ends(drawn, stream_key, low, high):
    longest = drawn.shape.index(max(drawn.shape))
    spots = []
    for shift in (0, 1):
        where = [jax.random.randint(jax.random.fold_in(stream_key, axis), (), 0, length) for axis, length in enumerate(drawn.shape)]
        where[longest] = (where[longest] + shift) % drawn.shape[longest]
        spots.append(tuple(where))
    return drawn.at[spots[0]].set(low).at[spots[1]].set(high)


def levels(rng, shape, cuts, low, top_value):
    factor_of, own = 1.0, jax.random.fold_in(rng, 6)
    for position, parts in cuts:
        draws = jnp.exp(jax.random.uniform(jax.random.fold_in(own, position), (parts,), jnp.float32, low / len(cuts), top_value / len(cuts)))
        factor_of = factor_of * jnp.repeat(draws, shape[position] // parts).reshape([-1 if axis == position else 1 for axis in range(len(shape))])
    return factor_of


def centred(rng, shape, width, most, shards=(), held_as=jnp.bfloat16):
    level = levels(rng, shape, shards, -0.22, 0.18) if shards else 1.0
    result = jax.random.normal(rng, shape, jnp.float32) * width * level
    return jnp.minimum(jnp.maximum(result, -most), most).astype(held_as)


def setup_inputs(seed: int = 0) -> dict:
    key_of = jax.random.split(jax.random.key(seed), 8)
    return {
        "blocks": centred(key_of[0], (BANDS, VISIT_BLOCKS, BLK, BLK), 1.0, 6.0, ((0, 4), (1, 8))),
        "dest_patch": draw_dest_patch(jax.random.fold_in(key_of[7], 71), 0),
        "dest_slot": touch_ends(jax.random.randint(key_of[2], (BANDS, VISIT_BLOCKS), 0, SLOTS), jax.random.fold_in(key_of[2], 1), 0, SLOTS - 1).astype(jnp.int32),
        "weights": jnp.clip(jnp.exp(math.log(4.0) - 2.7725887 * jax.random.uniform(key_of[3], (BANDS, VISIT_BLOCKS), jnp.float32) ** levels(key_of[3], (BANDS, VISIT_BLOCKS), ((0, 4), (1, 8)), -0.2, 0.2)), 0.25, 4.0).astype(jnp.bfloat16),
        "psf_taps": centred(key_of[4], (BANDS, VISIT_BLOCKS, 2, TAPS), TAPS ** -0.5, 1.0, ((0, 4), (1, 8))),
        "det_taps": centred(key_of[5], (BANDS, DTAPS), DTAPS ** -0.5, 1.25, ((0, 4),), jnp.float32),
        "noise_var": jnp.clip(jnp.exp(math.log(2.0) - 1.3862944 * jax.random.uniform(key_of[6], (BANDS,), jnp.float32) ** levels(key_of[6], (BANDS,), ((0, 4),), -0.2, 0.2)), 0.5, 2.0),
    }


def shift_table(kernel, number, extent):
    tap_count = kernel.shape[-1]
    leading = kernel.shape[:-1]
    padded_taps = jnp.concatenate([kernel, jnp.zeros(leading + (extent - tap_count + 1,), kernel.dtype)], axis=-1)
    repeated = jnp.tile(padded_taps, (1,) * len(leading) + (number,))
    return repeated[..., : number * extent].reshape(leading + (number, extent))


def band_rows(kernel, number):
    half_width = kernel.shape[-1] // 2
    table = shift_table(kernel, number, number + 2 * half_width)
    return table[..., :, half_width: half_width + number]


def match_group(grouped):
    group_blocks, group_taps = grouped
    matrices = band_rows(group_taps.astype(jnp.float32), BLK)
    half_pass = jnp.einsum("nij,njk->nik", matrices[:, 0], group_blocks.astype(jnp.float32)).astype(jnp.bfloat16)
    return jnp.einsum("nij,nkj->nik", half_pass.astype(jnp.float32), matrices[:, 1]).astype(jnp.bfloat16)


def reference(blocks, dest_patch, dest_slot, weights, psf_taps, det_taps, noise_var):
    npatch = VISIT_BLOCKS // VB_DEV
    groups = VISIT_BLOCKS // 4
    chi_total = jnp.zeros((PH, WIDTH), jnp.float32)
    images = []
    for band_index in range(BANDS):
        matched = lax.map(match_group, (blocks[band_index].reshape(groups, 4, BLK, BLK), psf_taps[band_index].reshape(groups, 4, 2, TAPS)))
        flattened = matched.reshape(VISIT_BLOCKS, BLK * BLK).astype(jnp.float32)
        target = dest_patch[band_index] * SLOTS + dest_slot[band_index]
        tile_picks = jnp.arange(npatch * SLOTS, dtype=jnp.int32)[:, None] == target[None, :]
        selected = jnp.where(tile_picks, weights[band_index].astype(jnp.float32)[None, :], jnp.zeros((), jnp.float32))
        weighted = jnp.dot(selected, flattened, precision=lax.Precision.HIGHEST)
        weight_sum = jnp.sum(selected, axis=1)
        tile_values = weighted / jnp.maximum(weight_sum, 1.0)[:, None]
        patch_image = tile_values.reshape(npatch, TH, TW, BLK, BLK).transpose(1, 3, 0, 2, 4).reshape(PH, WIDTH)
        images.append(patch_image)
        kernel = det_taps[band_index]
        col_pass = jnp.zeros((PH, WIDTH), jnp.float32)
        for offset in range(DTAPS):
            col_pass = col_pass + kernel[offset] * jnp.roll(patch_image, DR - offset, axis=1)
        padded = jnp.pad(col_pass, ((DR, DR), (0, 0)))
        row_pass = jnp.zeros((PH, WIDTH), jnp.float32)
        for offset in range(DTAPS):
            row_pass = row_pass + kernel[offset] * padded[offset: offset + PH]
        chi_total = chi_total + row_pass * row_pass / noise_var[band_index]
    return jnp.stack(images, axis=0), chi_total
```

```python
import jax
import jax.numpy as jnp
import numpy as np
from jax import lax
from jax.experimental import pallas as pl
from jax.experimental.pallas import tpu as pltpu
from jax.sharding import PartitionSpec as P

TH = 2
TW = 2
DR = 12
CAP = 4
SLOTS = 4
PAD = 16
DIGITS = 16
UNIT = 512


def dest_table(outer):
    table = np.zeros((outer, outer), np.int32)
    for z in range(outer):
        def due(d):
            if d > z:
                return (outer - 1 + z - d, 0)
            if d < z:
                return (outer - 1 - z + d, 1)
            return (outer, 0)

        table[z] = sorted(range(outer), key=due)
    return table


def toeplitz(row):
    half = row.shape[1] // 2
    wide = jnp.broadcast_to(row, (half, 2 * half))
    skew = pltpu.roll(wide, 0, 1, stride=1, stride_axis=0)
    diag = skew[:, :half]
    off = skew[:, half:]
    i = lax.broadcasted_iota(jnp.int32, (half, half), 0)
    j = lax.broadcasted_iota(jnp.int32, (half, half), 1)
    upper = jnp.where(j < i, off, 0.0)
    lower = jnp.where(j > i, off, 0.0)
    top = jnp.concatenate([diag, upper], axis=1)
    bottom = jnp.concatenate([lower, diag], axis=1)
    return jnp.concatenate([top, bottom], axis=0).astype(jnp.bfloat16)


def match_kernel(npatch, lists, order, blocks, taps, *rest):
    outs = rest[:npatch]
    acc, pay, edges, digits, count, index, sems = rest[npatch:]
    number, edge = blocks.shape[0], blocks.shape[-1]
    ntaps = taps.shape[-1]
    side = TH * edge

    def clear(p, carry):
        count[p] = 0
        for r in range(CAP):
            index[p * CAP + r] = -1
        return carry

    lax.fori_loop(0, npatch, clear, 0)

    def place(n, carry):
        p = lists[0, n]
        r = count[p]
        count[p] = r + 1
        index[p * CAP + r] = n
        return carry

    lax.fori_loop(0, number, place, 0)

    lane = lax.broadcasted_iota(jnp.int32, (8, 128), 1)

    def patch(k, carry):
        p = order[k]
        acc[...] = jnp.zeros(acc.shape, acc.dtype)
        row = jnp.zeros((8, 128), jnp.float32)
        for r in range(CAP):
            found = index[p * CAP + r]
            n = jnp.maximum(found, 0)
            s = lists[1, n]
            units = jnp.where(found >= 0, lists[2, n], 0)
            w = units.astype(jnp.float32) * (1.0 / UNIT)
            tap = taps[n].astype(jnp.float32)
            tap = jnp.concatenate([tap, jnp.zeros((2, edge - ntaps), jnp.float32)], axis=1)
            tap = pltpu.roll(tap, edge - ntaps // 2, 1)
            col = toeplitz(tap[0:1])
            half = jnp.dot(col, blocks[n], preferred_element_type=jnp.float32).astype(jnp.bfloat16)
            rowm = toeplitz(tap[1:2])
            matched = lax.dot_general(
                rowm, half, (((1,), (1,)), ((), ())), preferred_element_type=jnp.float32
            ).astype(jnp.bfloat16)
            acc[s] = acc[s] + w * matched.astype(jnp.float32)
            bit = lax.shift_right_logical(jnp.full((8, 128), units), lane % DIGITS) & 1
            row = row + jnp.where(lane // DIGITS == s, bit, 0).astype(jnp.float32)
        digits[p] = row
        for s in range(SLOTS):
            top = (s % TW) * edge
            left = (s // TW) * edge
            pay[k, PAD + top : PAD + top + edge, left : left + edge] = acc[s].astype(jnp.bfloat16)
        edges[p, 0] = pay[k, PAD : 2 * PAD, :]
        edges[p, 1] = pay[k, side : side + PAD, :]
        return carry

    lax.fori_loop(0, npatch, patch, 0)

    first = lax.broadcasted_iota(jnp.int32, (PAD, side), 0) == 0
    for k in range(npatch):
        p = order[k]
        before = lax.rem(p + npatch - 1, npatch)
        after = lax.rem(p + 1, npatch)
        row = jnp.concatenate(
            [digits[p], digits[before], digits[after], jnp.zeros((8, side - 3 * 128), jnp.float32)],
            axis=1,
        )
        row = jnp.concatenate([row, row], axis=0)
        pay[k, :PAD, :] = jnp.where(first, row, edges[before, 1].astype(jnp.float32)).astype(jnp.bfloat16)
        pay[k, PAD + side :, :] = edges[after, 0]
        pltpu.make_async_copy(pay.at[k], outs[k], sems.at[k]).start()
    for k in range(npatch):
        pltpu.make_async_copy(pay.at[k], outs[k], sems.at[k]).wait()


def match_blocks(lists, order, blocks, taps):
    npatch = order.shape[0]
    edge = blocks.shape[-1]
    side = TH * edge
    rows = side + 2 * PAD
    smem = pl.BlockSpec(memory_space=pltpu.SMEM)
    vmem = pl.BlockSpec(memory_space=pltpu.VMEM)
    return pl.pallas_call(
        lambda *refs: match_kernel(npatch, *refs),
        out_shape=[jax.ShapeDtypeStruct((rows, side), jnp.bfloat16)] * npatch,
        in_specs=[smem] * 2 + [vmem] * 2,
        out_specs=[pl.BlockSpec(memory_space=pl.ANY)] * npatch,
        scratch_shapes=[
            pltpu.VMEM((SLOTS, edge, edge), jnp.float32),
            pltpu.VMEM((npatch, rows, side), jnp.bfloat16),
            pltpu.VMEM((npatch, 2, PAD, side), jnp.bfloat16),
            pltpu.VMEM((npatch, 8, 128), jnp.float32),
            pltpu.SMEM((npatch,), jnp.int32),
            pltpu.SMEM((npatch * CAP,), jnp.int32),
            pltpu.SemaphoreType.DMA((npatch,)),
        ],
        compiler_params=pltpu.CompilerParams(vmem_limit_bytes=48 * 1024 * 1024),
        name="match",
    )(lists, order, blocks, taps)


def split(value):
    high = value.astype(jnp.bfloat16)
    return high, (value - high.astype(jnp.float32)).astype(jnp.bfloat16)


def dot3(ah, al, bh, bl, dims):
    def one(a, b):
        return lax.dot_general(a, b, (dims, ((), ())), preferred_element_type=jnp.float32)

    return one(ah, bh) + (one(ah, bl) + one(al, bh))


def tail_kernel(own, other, up, down, noise, colh, coll, rowh, rowl, image, chi):
    f32 = jnp.float32
    side = image.shape[0]
    edge = side // TH
    total = own[...].astype(f32) + other[...].astype(f32) + (up[...].astype(f32) + down[...].astype(f32))
    row = total[0:1, :]
    lane = lax.broadcasted_iota(jnp.int32, (1, side), 1)
    value = row * lax.shift_left(jnp.ones((1, side), jnp.int32), lane % DIGITS).astype(f32) * (1.0 / UNIT)

    def scale(group, s):
        here = (lane >= group * 128 + s * DIGITS) & (lane < group * 128 + (s + 1) * DIGITS)
        weight_sum = jnp.sum(jnp.where(here, value, 0.0), axis=1, keepdims=True)
        return jnp.broadcast_to(1.0 / jnp.maximum(weight_sum, 1.0), (1, edge))

    def factors(group, column):
        return jnp.concatenate([scale(group, r * TW + column) for r in range(TH)], axis=1)

    parts = [total[:PAD] * factors(1, TW - 1)]
    for column in range(TW):
        parts.append(total[PAD + column * edge : PAD + (column + 1) * edge] * factors(0, column))
    parts.append(total[PAD + side :] * factors(2, 0))
    padded = jnp.concatenate(parts, axis=0)
    image[...] = padded[PAD : PAD + side].T
    ph, plo = split(padded)
    col_pass = dot3(colh[...], coll[...], ph, plo, ((1,), (0,)))
    ch, cl = split(col_pass)
    row_pass = dot3(rowh[...], rowl[...], ch, cl, ((1,), (1,)))
    chi[...] = row_pass * row_pass * (1.0 / noise[0])


def tables_kernel(det, colh, coll, rowh, rowl):
    for high, low, start in ((colh, coll, DR - PAD), (rowh, rowl, DR)):
        offsets = (
            lax.broadcasted_iota(jnp.int32, high.shape, 1)
            - lax.broadcasted_iota(jnp.int32, high.shape, 0)
            + start
        )
        table = jnp.zeros(high.shape, jnp.float32)
        for tap in range(det.shape[1]):
            table = jnp.where(offsets == tap, det[0, tap], table)
        high[...], low[...] = split(table)


def filter_tables(det, rows, side):
    return pl.pallas_call(
        tables_kernel,
        out_shape=[jax.ShapeDtypeStruct(s, jnp.bfloat16) for s in [(side, rows)] * 2 + [(side, side)] * 2],
        in_specs=[pl.BlockSpec(memory_space=pltpu.SMEM)],
        out_specs=[pl.BlockSpec(memory_space=pltpu.VMEM)] * 4,
        compiler_params=pltpu.CompilerParams(vmem_limit_bytes=40 * 1024 * 1024),
        cost_estimate=pl.CostEstimate(flops=20_000_000, bytes_accessed=2_000_000, transcendentals=0),
        name="tables",
    )(det)


def finish(own, other, up, down, noise, det):
    rows, side = own.shape
    colh, coll, rowh, rowl = filter_tables(det, rows, side)
    smem = pl.BlockSpec(memory_space=pltpu.SMEM)
    vmem = pl.BlockSpec(memory_space=pltpu.VMEM)
    return pl.pallas_call(
        tail_kernel,
        out_shape=[jax.ShapeDtypeStruct((side, side), jnp.float32)] * 2,
        in_specs=[vmem] * 4 + [smem] + [vmem] * 4,
        out_specs=[vmem] * 2,
        compiler_params=pltpu.CompilerParams(vmem_limit_bytes=40 * 1024 * 1024),
        name="finish",
    )(own, other, up, down, noise, colh, coll, rowh, rowl)


def local(blocks, dest_patch, dest_slot, weights, psf_taps, det_taps, noise_var):
    f32, bf16 = jnp.float32, jnp.bfloat16
    npatch = lax.axis_size("patch")
    outer = npatch // 2
    me = lax.axis_index("patch")
    z = me // 2
    table = dest_table(outer)
    where_is = np.argsort(table, axis=1)
    order = np.zeros((npatch, npatch), np.int32)
    for i in range(npatch):
        for s in range(outer):
            order[i, 2 * s] = table[i // 2, s] * 2 + 1 - i % 2
            order[i, 2 * s + 1] = table[i // 2, s] * 2 + i % 2
    order = lax.dynamic_index_in_dim(jnp.asarray(order), me, 0, keepdims=False)
    units = (weights.astype(f32) * UNIT).astype(jnp.int32)
    lists = jnp.concatenate([dest_patch, dest_slot, units], axis=0)
    payloads = match_blocks(lists, order, blocks[0], psf_taps[0])
    swap = [(i, i ^ 1) for i in range(npatch)]
    kept = []
    for s in range(outer):
        other = lax.ppermute(payloads[2 * s], "patch", swap)
        kept.append((payloads[2 * s + 1], other))

    def combined(s):
        return kept[s][0].astype(f32) + kept[s][1].astype(f32)

    def chosen(places):
        values = sorted(set(places.values()))
        result = combined(values[-1])
        for v in values[:-1]:
            mine = functools_any([z == q for q, s in places.items() if s == v])
            result = jnp.where(mine, combined(v), result)
        return result

    up = down = None
    for t in range(outer - 1):
        up_places = {q: int(where_is[q][outer - 1 - t + q]) for q in range(t + 1)}
        down_places = {outer - 1 - q: int(where_is[outer - 1 - q][t - q]) for q in range(t + 1)}
        send_up = chosen(up_places)
        send_down = chosen(down_places)
        if up is not None:
            send_up = send_up + up.astype(f32)
            send_down = send_down + down.astype(f32)
        up_pairs = [(2 * q + y, 2 * q + 2 + y) for q in range(t + 1) for y in range(2)]
        down_pairs = [(npatch - 1 - a, npatch - 1 - b) for a, b in up_pairs]
        up = lax.ppermute(send_up.astype(bf16), "patch", up_pairs)
        down = lax.ppermute(send_down.astype(bf16), "patch", down_pairs)
    image, term = finish(kept[-1][0], kept[-1][1], up, down, noise_var, det_taps)
    band = lax.axis_index("band")
    rows = term.shape[0] // 4
    chunks = term.reshape(2, 2, rows, term.shape[1])
    core, far = band % 2, band // 2
    mine = lax.dynamic_index_in_dim(chunks, core, 1, keepdims=False)
    theirs = lax.dynamic_index_in_dim(chunks, 1 - core, 1, keepdims=False)
    pair = mine + lax.ppermute(theirs, "band", [(i, i ^ 1) for i in range(4)])
    mine = lax.dynamic_index_in_dim(pair, far, 0, keepdims=False)
    theirs = lax.dynamic_index_in_dim(pair, 1 - far, 0, keepdims=False)
    chi = mine + lax.ppermute(theirs, "band", [(i, i ^ 2) for i in range(4)])
    return image[None], chi


def functools_any(flags):
    result = flags[0]
    for flag in flags[1:]:
        result = result | flag
    return result


def solution(mesh):
    in_specs = (
        P("band", "patch", None, None),
        P("band", "patch"),
        P("band", "patch"),
        P("band", "patch"),
        P("band", "patch", None, None),
        P("band", None),
        P("band"),
    )
    out_specs = (P("band", None, "patch"), P("band", "patch"))
    return jax.shard_map(local, mesh=mesh, in_specs=in_specs, out_specs=out_specs, check_vma=False)
```

```python
import jax
import jax.numpy as jnp
import numpy as np
from jax import lax
from jax.experimental import pallas as pl
from jax.experimental.pallas import tpu as pltpu
from jax.sharding import PartitionSpec as P

TH = 2
TW = 2
DR = 12
CAP = 4
SLOTS = 4
PAD = 16
DIGITS = 16
UNIT = 512


def dest_table(outer):
    table = np.zeros((outer, outer), np.int32)
    for z in range(outer):
        def due(d):
            if d > z:
                return (outer - 1 + z - d, d == z ^ 1)
            if d < z:
                return (outer - 1 - z + d, d == z ^ 1)
            return (outer, 0)

        table[z] = sorted(range(outer), key=due)
    return table


def toeplitz(row):
    half = row.shape[1] // 2
    wide = jnp.broadcast_to(row, (half, 2 * half))
    skew = pltpu.roll(wide, 0, 1, stride=1, stride_axis=0)
    diag = skew[:, :half]
    off = skew[:, half:]
    i = lax.broadcasted_iota(jnp.int32, (half, half), 0)
    j = lax.broadcasted_iota(jnp.int32, (half, half), 1)
    upper = jnp.where(j < i, off, 0.0)
    lower = jnp.where(j > i, off, 0.0)
    top = jnp.concatenate([diag, upper], axis=1)
    bottom = jnp.concatenate([lower, diag], axis=1)
    return jnp.concatenate([top, bottom], axis=0).astype(jnp.bfloat16)


def make_lists(npatch, dest, count, index):
    def clear(p, carry):
        count[p] = 0
        for r in range(CAP):
            index[p * CAP + r] = -1
        return carry

    lax.fori_loop(0, npatch, clear, 0)

    def place(n, carry):
        p = dest[0, n]
        r = count[p]
        count[p] = r + 1
        index[p * CAP + r] = n
        return carry

    lax.fori_loop(0, dest.shape[1], place, 0)


def match_patch(p, q, k, slot, units, index, block, taps, acc, pay, edges, digits):
    edge = acc.shape[-1]
    ntaps = taps.shape[-1]
    side = TH * edge
    lane = lax.broadcasted_iota(jnp.int32, (8, 128), 1)
    acc[...] = jnp.zeros(acc.shape, acc.dtype)
    row = jnp.zeros((8, 128), jnp.float32)
    for r in range(CAP):
        found = index[p * CAP + r]
        n = jnp.maximum(found, 0)
        s = slot[0, n]
        unit = jnp.where(found >= 0, units[0, n], 0)
        w = unit.astype(jnp.float32) * (1.0 / UNIT)
        tap = taps[n].astype(jnp.float32)
        tap = jnp.concatenate([tap, jnp.zeros((2, edge - ntaps), jnp.float32)], axis=1)
        tap = pltpu.roll(tap, edge - ntaps // 2, 1)
        col = toeplitz(tap[0:1])
        half = jnp.dot(col, block(n, r), preferred_element_type=jnp.float32).astype(jnp.bfloat16)
        rowm = toeplitz(tap[1:2])
        matched = lax.dot_general(
            rowm, half, (((1,), (1,)), ((), ())), preferred_element_type=jnp.float32
        ).astype(jnp.bfloat16)
        acc[s] = acc[s] + w * matched.astype(jnp.float32)
        bit = lax.shift_right_logical(jnp.full((8, 128), unit), lane % DIGITS) & 1
        row = row + jnp.where(lane // DIGITS == s, bit, 0).astype(jnp.float32)
    digits[q] = row
    for s in range(SLOTS):
        top = (s % TW) * edge
        left = (s // TW) * edge
        pay[k, PAD + top : PAD + top + edge, left : left + edge] = acc[s].astype(jnp.bfloat16)
    edges[q, 0] = pay[k, PAD : 2 * PAD, :]
    edges[q, 1] = pay[k, side : side + PAD, :]


def add_halos(k, before, q, after, pay, edges, digits):
    rows, side = pay.shape[1:]
    first = lax.broadcasted_iota(jnp.int32, (PAD, side), 0) == 0
    blank = jnp.zeros((8, side - 3 * 128), jnp.float32)
    row = jnp.concatenate([digits[q], digits[before], digits[after], blank], axis=1)
    row = jnp.concatenate([row, row], axis=0)
    pay[k, :PAD, :] = jnp.where(first, row, edges[before, 1].astype(jnp.float32)).astype(jnp.bfloat16)
    pay[k, rows - PAD :, :] = edges[after, 0]


def first_kernel(
    npatch, dest_in, slot_in, weights_in, blocks_in, taps_in,
    s_a, k_a, s_b, k_b, own, edges, digits, dest, slot, units,
    acc, pay, blocks, taps, weights, wide, count, index, sems, sends,
):
    fetched = [
        pltpu.make_async_copy(dest_in, dest, sems.at[0]),
        pltpu.make_async_copy(weights_in, weights, sems.at[1]),
        pltpu.make_async_copy(slot_in, slot, sems.at[2]),
        pltpu.make_async_copy(taps_in, taps, sems.at[3]),
        pltpu.make_async_copy(blocks_in, blocks, sems.at[4]),
    ]
    for copy in fetched:
        copy.start()
    fetched[1].wait()
    wide[...] = (weights[...].astype(jnp.float32) * UNIT).astype(jnp.int32)
    convert = pltpu.make_async_copy(wide, units, sems.at[5])
    convert.start()
    me = lax.axis_index("patch")
    base = jnp.where(2 * (me // 2) < npatch // 2, npatch - 3, npatch - 1)
    fetched[0].wait()
    make_lists(npatch, dest, count, index)
    convert.wait()
    for copy in fetched[2:]:
        copy.wait()

    rows, side = pay.shape[1:]
    half = rows // 2
    copies = []

    def send(source, out):
        copies.append(pltpu.make_async_copy(source, out, sends.at[len(copies)]))
        copies[-1].start()

    def either_way(first_out, second_out, q, part):
        source = pay.at[q, part * half : (part + 1) * half]
        copy = [pltpu.make_async_copy(source, out, sends.at[len(copies)]) for out in (first_out, second_out)]
        copies.append(copy[0])
        goes = lax.rem(me, 2) == 2 - q
        pl.when(goes)(copy[0].start)
        pl.when(jnp.logical_not(goes))(copy[1].start)

    for q in range(4):
        p = lax.rem(base + q, npatch)
        match_patch(p, q, q, slot, units, index, lambda n, r: blocks[n], taps, acc, pay, edges, digits)
        if q > 1:
            add_halos(q - 1, q - 2, q - 1, q, pay, edges, digits)
            either_way(s_a, k_a, q - 1, 0)
            either_way(s_b, k_b, q - 1, 1)
        if q % 3 == 0:
            send(pay.at[q, PAD : PAD + side], own.at[q // 3])
    for copy in copies:
        copy.wait()


def make_turns(outer):
    last = outer - 1
    turns = [[(0, 0)], [(0, 1)], [(1, 0)]]
    turns += [[(s, 0), (s - 1, 1)] for s in range(2, last)]
    return turns + [[(last - 1, 1)], [(last, 0)], [(last, 1)]]


def rest_kernel(npatch, dest, slot, units, order, blocks_in, taps, own, edges0, digits0, *rest):
    turns = make_turns(npatch // 2)[2:]
    outs = rest[: len(turns) + npatch - 2]
    acc, pay, blocks, edges, digits, count, index, place, sems, sends = rest[len(turns) + npatch - 2 :]
    sent = {part: (turn, i) for turn, parts in enumerate(turns) for i, part in enumerate(parts)}
    rows, side = pay.shape[1:]
    half = rows // 2
    base = (order[0] // 2) * 2 + npatch - 1
    fetch = pltpu.make_async_copy(blocks_in, blocks, sems.at[2])
    fetch.start()

    def put(k, carry):
        place[order[k]] = k - 2
        return carry

    lax.fori_loop(0, npatch, put, 0)
    given = []
    for j in range(2):
        k = place[lax.rem(base + 3 * j, npatch)]
        given.append(pltpu.make_async_copy(own.at[j], pay.at[k, PAD : PAD + side], sems.at[j]))
        given[-1].start()
    make_lists(npatch, dest, count, index)
    for q in range(4):
        edges[q] = edges0[q]
        digits[q] = digits0[q]

    def copies(k):
        result = []
        for j in range(2):
            if k % 2:
                out = outs[len(turns) + k - 1 + j]
            else:
                turn, i = sent[k // 2 + 1, j]
                out = outs[turn].at[i * half : (i + 1) * half]
            result.append(pltpu.make_async_copy(pay.at[k, j * half : (j + 1) * half], out, sends.at[2 * k + j]))
        return result

    def send(q):
        mine = place[lax.rem(base + q, npatch)]
        add_halos(mine, lax.rem(q + npatch - 1, npatch), q, lax.rem(q + 1, npatch), pay, edges, digits)
        for k in range(npatch - 2):

            @pl.when(mine == k)
            def _():
                for copy in copies(k):
                    copy.start()

    given[0].wait()
    given[1].wait()
    fetch.wait()

    def patch(q, carry):
        p = lax.rem(base + q, npatch)
        match_patch(p, q, place[p], slot, units, index, lambda n, r: blocks[n], taps, acc, pay, edges, digits)
        send(q - 1)
        return carry

    lax.fori_loop(4, npatch, patch, 0, unroll=2)
    send(npatch - 1)
    send(0)
    for k in range(npatch - 2):
        for copy in copies(k):
            copy.wait()


def match_blocks(dest, slot, weights, orders, blocks, taps):
    npatch, number = orders.shape[0], blocks.shape[0]
    edge = blocks.shape[-1]
    side = TH * edge
    rows = side + 2 * PAD
    smem = pl.BlockSpec(memory_space=pltpu.SMEM)
    vmem = pl.BlockSpec(memory_space=pltpu.VMEM)
    hbm = pl.BlockSpec(memory_space=pltpu.HBM)
    half = jax.ShapeDtypeStruct((rows // 2, side), jnp.bfloat16)
    acc = pltpu.VMEM((SLOTS, edge, edge), jnp.float32)
    params = pltpu.CompilerParams(vmem_limit_bytes=64 * 1024 * 1024)
    count = pltpu.SMEM((npatch,), jnp.int32)
    index = pltpu.SMEM((npatch * CAP,), jnp.int32)
    s_a, k_a, s_b, k_b, own, edges, digits, dest, slot, units = pl.pallas_call(
        lambda *refs: first_kernel(npatch, *refs),
        out_shape=[half] * 4
        + [
            jax.ShapeDtypeStruct((2, side, side), jnp.bfloat16),
            jax.ShapeDtypeStruct((4, 2, PAD, side), jnp.bfloat16),
            jax.ShapeDtypeStruct((4, 8, 128), jnp.float32),
        ]
        + [jax.ShapeDtypeStruct((1, number), jnp.int32)] * 3,
        in_specs=[hbm] * 5,
        out_specs=[hbm] * 5 + [vmem] * 2 + [smem] * 3,
        scratch_shapes=[
            acc,
            pltpu.VMEM((4, rows, side), jnp.bfloat16),
            pltpu.VMEM(blocks.shape, jnp.bfloat16),
            pltpu.VMEM(taps.shape, jnp.bfloat16),
            pltpu.VMEM((1, number), jnp.bfloat16),
            pltpu.VMEM((1, number), jnp.int32),
            count,
            index,
            pltpu.SemaphoreType.DMA((6,)),
            pltpu.SemaphoreType.DMA((6,)),
        ],
        compiler_params=params,
        name="match_first",
    )(dest, slot, weights, blocks, taps)
    me, _ = lax.optimization_barrier((lax.axis_index("patch"), s_a))
    order = lax.dynamic_index_in_dim(jnp.asarray(orders), me, 0, keepdims=False)
    turns = make_turns(npatch // 2)
    outs = pl.pallas_call(
        lambda *refs: rest_kernel(npatch, *refs),
        out_shape=[jax.ShapeDtypeStruct((rows // 2 * len(turn), side), jnp.bfloat16) for turn in turns[2:]]
        + [half] * (npatch - 2),
        in_specs=[smem] * 4 + [hbm, vmem, hbm, vmem, vmem],
        out_specs=[hbm] * (len(turns) - 2 + npatch - 2),
        scratch_shapes=[
            acc,
            pltpu.VMEM((npatch - 2, rows, side), jnp.bfloat16),
            pltpu.VMEM(blocks.shape, jnp.bfloat16),
            pltpu.VMEM((npatch, 2, PAD, side), jnp.bfloat16),
            pltpu.VMEM((npatch, 8, 128), jnp.float32),
            count,
            index,
            pltpu.SMEM((npatch,), jnp.int32),
            pltpu.SemaphoreType.DMA((3,)),
            pltpu.SemaphoreType.DMA((2 * (npatch - 2),)),
        ],
        compiler_params=params,
        cost_estimate=pl.CostEstimate(flops=2_000_000_000, bytes_accessed=8_000_000, transcendentals=0),
        name="match_rest",
    )(dest, slot, units, order, blocks, taps, own, edges, digits)
    sends = [s_a, s_b] + list(outs[: len(turns) - 2])
    kept = outs[len(turns) - 2 :]
    return sends, [(k_a, k_b)] + [(kept[2 * k], kept[2 * k + 1]) for k in range(npatch // 2 - 1)]


def split(value):
    high = value.astype(jnp.bfloat16)
    return high, (value - high.astype(jnp.float32)).astype(jnp.bfloat16)


def dot3(ah, al, bh, bl, dims):
    def one(a, b):
        return lax.dot_general(a, b, (dims, ((), ())), preferred_element_type=jnp.float32)

    return one(ah, bh) + (one(ah, bl) + one(al, bh))


def chi_rows(place, rowh, rowl, ch, cl, noise):
    rows = pl.ds(pl.multiple_of(place * 128, 128), 128)
    row_pass = dot3(rowh[rows, :], rowl[rows, :], ch, cl, ((1,), (1,)))
    return row_pass * row_pass * (1.0 / noise[0])


def total(x0, x1, x2, x3):
    f32 = jnp.float32
    return x0[...].astype(f32) + x1[...].astype(f32) + (x2[...].astype(f32) + x3[...].astype(f32))


def tail_left(a0, a1, a2, a3, colh, coll, normed, part, factor):
    f32 = jnp.float32
    half, side = a0.shape
    edge = side // TH
    left = total(a0, a1, a2, a3)
    lane = lax.broadcasted_iota(jnp.int32, (1, side), 1)
    power = lax.shift_left(jnp.ones((1, side), jnp.int32), lane % DIGITS).astype(f32) * (1.0 / UNIT)
    value = left[0:1, :] * power

    def scale(group, s):
        here = (lane >= group * 128 + s * DIGITS) & (lane < group * 128 + (s + 1) * DIGITS)
        weight_sum = jnp.sum(jnp.where(here, value, 0.0), axis=1, keepdims=True)
        return jnp.broadcast_to(1.0 / jnp.maximum(weight_sum, 1.0), (1, edge))

    def factors(group, column):
        return jnp.concatenate([scale(group, r * TW + column) for r in range(TH)], axis=1)

    left = jnp.concatenate([left[:PAD] * factors(1, TW - 1), left[PAD:] * factors(0, 0)], axis=0)
    normed[...] = left[PAD:]
    high, low = split(left)
    part[...] = dot3(colh[:, :half], coll[:, :half], high, low, ((1,), (0,)))
    factor[0] = jnp.broadcast_to(factors(0, 1), (8, side))
    factor[1] = jnp.broadcast_to(factors(2, 0), (8, side))


def tail_right(
    b0, b1, b2, b3, factor, part, noise, band, colh, coll, rowh, rowl, normed, give, stay
):
    half, side = b0.shape
    edge = side // TH
    right = total(b0, b1, b2, b3)
    right = jnp.concatenate([right[:edge] * factor[0, 0:1], right[edge:] * factor[1, 0:1]], axis=0)
    normed[...] = right[:edge]
    high, low = split(right)
    ch, cl = split(part[...] + dot3(colh[:, half:], coll[:, half:], high, low, ((1,), (0,))))
    for j, place in enumerate((band[0], band[0] ^ 2)):
        give[j] = chi_rows(place ^ 1, rowh, rowl, ch, cl, noise)
        stay[j] = chi_rows(place, rowh, rowl, ch, cl, noise)


def tail_image(left, right, image):
    edge = left.shape[0]
    image[:, :edge] = left[...].T
    image[:, edge:] = right[...].T


def tables_kernel(det, colh, coll, rowh, rowl):
    for high, low, start in ((colh, coll, DR - PAD), (rowh, rowl, DR)):
        offsets = (
            lax.broadcasted_iota(jnp.int32, high.shape, 1)
            - lax.broadcasted_iota(jnp.int32, high.shape, 0)
            + start
        )
        table = jnp.zeros(high.shape, jnp.float32)
        for tap in range(det.shape[1]):
            table = jnp.where(offsets == tap, det[0, tap], table)
        high[...], low[...] = split(table)


def filter_tables(det, rows, side):
    return pl.pallas_call(
        tables_kernel,
        out_shape=[jax.ShapeDtypeStruct(s, jnp.bfloat16) for s in [(side, rows)] * 2 + [(side, side)] * 2],
        in_specs=[pl.BlockSpec(memory_space=pltpu.SMEM)],
        out_specs=[pl.BlockSpec(memory_space=pltpu.VMEM)] * 4,
        compiler_params=pltpu.CompilerParams(vmem_limit_bytes=40 * 1024 * 1024),
        cost_estimate=pl.CostEstimate(flops=20_000_000, bytes_accessed=2_000_000, transcendentals=0),
        name="tables",
    )(det)


def finish(left, right, noise, det):
    rows, side = left[0].shape[0] * 2, left[0].shape[1]
    f32, bf16 = jnp.float32, jnp.bfloat16
    colh, coll, rowh, rowl = filter_tables(det, rows, side)
    band = lax.axis_index("band")
    where = band.reshape(1).astype(jnp.int32)
    smem = pl.BlockSpec(memory_space=pltpu.SMEM)
    vmem = pl.BlockSpec(memory_space=pltpu.VMEM)
    params = pltpu.CompilerParams(vmem_limit_bytes=40 * 1024 * 1024)
    quarters = jax.ShapeDtypeStruct((2, side // 4, side), f32)
    whole = jax.ShapeDtypeStruct((side, side), f32)
    tile = jax.ShapeDtypeStruct((side // TW, side), f32)
    normed_left, part, factor = pl.pallas_call(
        tail_left,
        out_shape=[tile, whole, jax.ShapeDtypeStruct((2, 8, side), f32)],
        in_specs=[vmem] * 6,
        out_specs=[vmem] * 3,
        compiler_params=params,
        cost_estimate=pl.CostEstimate(flops=500_000_000, bytes_accessed=4_000_000, transcendentals=0),
        name="tail_left",
    )(*left, colh, coll)
    normed_right, give, stay = pl.pallas_call(
        tail_right,
        out_shape=[tile, quarters, quarters],
        in_specs=[vmem] * 6 + [smem] * 2 + [vmem] * 4,
        out_specs=[vmem] * 3,
        compiler_params=params,
        name="tail_right",
    )(*right, factor, part, noise, where, colh, coll, rowh, rowl)
    pair = stay + lax.ppermute(give, "band", [(i, i ^ 1) for i in range(4)])
    beyond = lax.ppermute(pair[1].astype(bf16), "band", [(i, i ^ 2) for i in range(4)])
    normed_right, _ = lax.optimization_barrier((normed_right, pair))
    image = pl.pallas_call(
        tail_image,
        out_shape=whole,
        in_specs=[vmem] * 2,
        out_specs=vmem,
        compiler_params=params,
        cost_estimate=pl.CostEstimate(flops=0, bytes_accessed=2_000_000, transcendentals=0),
        name="tail_image",
    )(normed_left, normed_right)
    return image, pair[0] + beyond.astype(f32)


def either(flags):
    result = flags[0]
    for flag in flags[1:]:
        result = result | flag
    return result


def local(blocks, dest_patch, dest_slot, weights, psf_taps, det_taps, noise_var):
    f32, bf16 = jnp.float32, jnp.bfloat16
    npatch = lax.axis_size("patch")
    outer = npatch // 2
    me = lax.axis_index("patch")
    z = me // 2
    table = dest_table(outer)
    where_is = np.argsort(table, axis=1)
    order = np.zeros((npatch, npatch), np.int32)
    for i in range(npatch):
        for s in range(outer):
            order[i, 2 * s] = table[i // 2, s] * 2 + 1 - i % 2
            order[i, 2 * s + 1] = table[i // 2, s] * 2 + i % 2
    sends, kept = match_blocks(dest_patch, dest_slot, weights, order, blocks[0], psf_taps[0])
    last = outer - 1
    nband = lax.axis_size("band")
    across = [(i, i ^ 1) for i in range(npatch)]
    even = [(i, i ^ 2) for i in range(npatch)]
    odd = []
    for i in range(npatch):
        q = i // 2
        to = q + 1 if q % 2 else q - 1
        for j in range(nband):
            if 0 <= to < outer:
                odd.append((i * nband + j, (2 * to + i % 2) * nband + j))
            else:
                odd.append((i * nband + j, i * nband + (j ^ 1)))
    came = {}
    got = []
    for i, (parts, send) in enumerate(zip(make_turns(outer), sends, strict=True)):
        if i > 2:
            send, _ = lax.optimization_barrier((send, got[i - 2] if i > 3 else got[0]))
        with jax.named_scope(f"across_turn_{i}_of"):
            got.append(lax.ppermute(send, "patch", across))
        for j, part in enumerate(parts):
            rows = got[-1].shape[0] // len(parts)
            came[part] = lax.slice_in_dim(got[-1], j * rows, (j + 1) * rows)

    def combined(s, c):
        return kept[s][c].astype(f32) + came[s, c].astype(f32)

    def chosen(places, c):
        values = sorted(set(places.values()))
        result = combined(values[-1], c)
        for v in values[:-1]:
            result = jnp.where(either([z == q for q, s in places.items() if s == v]), combined(v, c), result)
        return result

    def step(t, parity, c):
        places = {}
        for q in range(outer):
            rising = q % 2 == parity
            hops = q if rising else last - q
            d = last - t + q if rising else t - hops
            if hops <= t and 0 <= d < outer and d != q:
                places[q] = int(where_is[q][d])
        return chosen(places, c)

    def masked(value, ends):
        return jnp.where(either([z == q for q in ends]), 0.0, value.astype(f32))

    evens, odds = [None, None], [None, None]
    for t in range(last):
        for c in range(2):
            send = step(t, 0, c)
            if t > 1:
                send = send + masked(odds[c], (0, last))
            send_odd = step(t, 1, c) + evens[c].astype(f32) if t else None
            side = "left" if c == 0 else "right"
            with jax.named_scope(f"even_step_{t}_{side}"):
                evens[c] = lax.ppermute(send.astype(bf16), "patch", even)
            if t == 1 and c == 1:
                det_taps, _ = lax.optimization_barrier((det_taps, evens[c]))
            if t:
                with jax.named_scope(f"odd_step_{t}_{side}"):
                    odds[c] = lax.ppermute(send_odd.astype(bf16), ("patch", "band"), odd)
    for c in range(2):
        odds[c] = masked(odds[c], (0, last)).astype(bf16)
    ends = [(kept[last][c], came[last, c], evens[c], odds[c]) for c in range(2)]
    image, chi = finish(*ends, noise_var, det_taps)
    return image[None], chi


def solution(mesh):
    in_specs = (
        P("band", "patch", None, None),
        P("band", "patch"),
        P("band", "patch"),
        P("band", "patch"),
        P("band", "patch", None, None),
        P("band", None),
        P("band"),
    )
    out_specs = (P("band", None, "patch"), P("band", "patch"))
    return jax.shard_map(local, mesh=mesh, in_specs=in_specs, out_specs=out_specs, check_vma=False)
```

```python
import jax
import jax.numpy as jnp
import numpy as np
from jax import lax
from jax.experimental import pallas as pl
from jax.experimental.pallas import tpu as pltpu
from jax.sharding import PartitionSpec as P

TH = 2
TW = 2
DR = 12
CAP = 4
SLOTS = 4
PAD = 16
DIGITS = 16
UNIT = 512


def cuts(rows):
    return (0, rows // 2 + PAD, rows)


def dest_table(outer):
    table = np.zeros((outer, outer), np.int32)
    for z in range(outer):
        def due(d):
            if d > z:
                return (outer - 1 + z - d, d == z ^ 1)
            if d < z:
                return (outer - 1 - z + d, d == z ^ 1)
            return (outer, 0)

        table[z] = sorted(range(outer), key=due)
    return table


def toeplitz(row):
    half = row.shape[1] // 2
    wide = jnp.broadcast_to(row, (half, 2 * half))
    skew = pltpu.roll(wide, 0, 1, stride=1, stride_axis=0)
    diag = skew[:, :half]
    off = skew[:, half:]
    i = lax.broadcasted_iota(jnp.int32, (half, half), 0)
    j = lax.broadcasted_iota(jnp.int32, (half, half), 1)
    upper = jnp.where(j < i, off, 0.0)
    lower = jnp.where(j > i, off, 0.0)
    top = jnp.concatenate([diag, upper], axis=1)
    bottom = jnp.concatenate([lower, diag], axis=1)
    return jnp.concatenate([top, bottom], axis=0).astype(jnp.bfloat16)


def make_lists(npatch, dest, count, index):
    def clear(p, carry):
        count[p] = 0
        for r in range(CAP):
            index[p * CAP + r] = -1
        return carry

    lax.fori_loop(0, npatch, clear, 0)

    def place(n, carry):
        p = dest[0, n]
        r = count[p]
        count[p] = r + 1
        index[p * CAP + r] = n
        return carry

    lax.fori_loop(0, dest.shape[1], place, 0)


def match_patch(p, q, k, slot, units, index, block, taps, acc, pay, edges, digits):
    edge = acc.shape[-1]
    ntaps = taps.shape[-1]
    side = TH * edge
    lane = lax.broadcasted_iota(jnp.int32, (8, 128), 1)
    acc[...] = jnp.zeros(acc.shape, acc.dtype)
    row = jnp.zeros((8, 128), jnp.float32)
    for r in range(CAP):
        found = index[p * CAP + r]
        n = jnp.maximum(found, 0)
        s = slot[0, n]
        unit = jnp.where(found >= 0, units[0, n], 0)
        w = unit.astype(jnp.float32) * (1.0 / UNIT)
        tap = taps[n].astype(jnp.float32)
        tap = jnp.concatenate([tap, jnp.zeros((2, edge - ntaps), jnp.float32)], axis=1)
        tap = pltpu.roll(tap, edge - ntaps // 2, 1)
        col = toeplitz(tap[0:1])
        half = jnp.dot(col, block(n, r), preferred_element_type=jnp.float32).astype(jnp.bfloat16)
        rowm = toeplitz(tap[1:2])
        matched = lax.dot_general(
            rowm, half, (((1,), (1,)), ((), ())), preferred_element_type=jnp.float32
        ).astype(jnp.bfloat16)
        acc[s] = acc[s] + w * matched.astype(jnp.float32)
        bit = lax.shift_right_logical(jnp.full((8, 128), unit), lane % DIGITS) & 1
        row = row + jnp.where(lane // DIGITS == s, bit, 0).astype(jnp.float32)
    digits[q] = row
    for s in range(SLOTS):
        top = (s % TW) * edge
        left = (s // TW) * edge
        pay[k, PAD + top : PAD + top + edge, left : left + edge] = acc[s].astype(jnp.bfloat16)
    edges[q, 0] = pay[k, PAD : 2 * PAD, :]
    edges[q, 1] = pay[k, side : side + PAD, :]


def add_halos(k, before, q, after, pay, edges, digits):
    rows, side = pay.shape[1:]
    first = lax.broadcasted_iota(jnp.int32, (PAD, side), 0) == 0
    blank = jnp.zeros((8, side - 3 * 128), jnp.float32)
    row = jnp.concatenate([digits[q], digits[before], digits[after], blank], axis=1)
    row = jnp.concatenate([row, row], axis=0)
    pay[k, :PAD, :] = jnp.where(first, row, edges[before, 1].astype(jnp.float32)).astype(jnp.bfloat16)
    pay[k, rows - PAD :, :] = edges[after, 0]


def begin(npatch, sources, targets, wide, units, count, index, sems):
    fetched = [pltpu.make_async_copy(x, y, sems.at[i]) for i, (x, y) in enumerate(zip(sources, targets, strict=True))]
    for copy in fetched:
        copy.start()
    dest, weights = targets[:2]
    fetched[1].wait()
    wide[...] = (weights[...].astype(jnp.float32) * UNIT).astype(jnp.int32)
    convert = pltpu.make_async_copy(wide, units, sems.at[len(fetched)])
    convert.start()
    fetched[0].wait()
    make_lists(npatch, dest, count, index)
    return [*fetched[2:], convert]


def base_of(npatch, me):
    return jnp.where(2 * (me // 2) < npatch // 2, npatch - 3, npatch - 1)


def first_kernel(
    npatch, dest_in, slot_in, weights_in, blocks_in, taps_in, s_a, k_a, both, own, edges_out, digits_out,
    acc, pay, blocks, taps, weights, wide, edges, digits, dest, slot, units, count, index, sems, sends,
):
    sources = (dest_in, weights_in, slot_in, taps_in, blocks_in)
    waits = begin(npatch, sources, (dest, weights, slot, taps, blocks), wide, units, count, index, sems)
    me = lax.axis_index("patch")
    base = base_of(npatch, me)
    for copy in waits:
        copy.wait()
    rows, side = pay.shape[1:]
    copies = []

    def send(source, out):
        copies.append(pltpu.make_async_copy(source, out, sends.at[len(copies)]))
        copies[-1].start()

    def either_way(first_out, second_out, q, part):
        source = pay.at[q, cuts(rows)[part] : cuts(rows)[part + 1]]
        copy = [pltpu.make_async_copy(source, out, sends.at[len(copies)]) for out in (first_out, second_out)]
        copies.append(copy[0])
        goes = lax.rem(me, 2) == 2 - q
        pl.when(goes)(copy[0].start)
        pl.when(jnp.logical_not(goes))(copy[1].start)

    def match(q):
        p = lax.rem(base + q, npatch)
        match_patch(p, q, q, slot, units, index, lambda n, r: blocks[n], taps, acc, pay, edges, digits)

    match(0)
    match(1)
    send(pay.at[0, PAD : PAD + side], own.at[0])
    match(2)
    match(3)
    height = both.shape[0] // 2
    for q in (1, 2):
        add_halos(q, q - 1, q, q + 1, pay, edges, digits)
        either_way(s_a, k_a, q, 0)
        either_way(both.at[:height], both.at[height:], q, 1)
    send(pay.at[3, PAD : PAD + side], own.at[1])
    send(edges, edges_out)
    send(digits, digits_out)
    for copy in copies:
        copy.wait()


def make_turns(outer):
    last = outer - 1
    turns = [[(0, 0)], [(1, 0)], [(1, 1)], [(last - 1, 1)]]
    turns += [[(s, 0), (s, 1)] for s in range(2, last - 1)]
    return turns + [[(last - 1, 0)], [(last, 0)], [(last, 1)]]


def rest_kernel(
    npatch, dest_in, slot_in, weights_in, blocks_in, taps_in, orders_in, own, edges_in, digits_in, *rest
):
    turns = make_turns(npatch // 2)[1:]
    sent = {part: turn for turn, parts in enumerate(turns) for part in parts}
    number = len(turns) + npatch - 2
    outs = rest[:number]
    (
        acc, pay, blocks, taps, weights, wide, edges, digits,
        dest, slot, units, orders, count, index, place, sems, sends,
    ) = rest[number:]
    sources = (dest_in, weights_in, orders_in, slot_in, taps_in, edges_in, digits_in, blocks_in)
    targets = (dest, weights, orders, slot, taps, edges.at[:4], digits.at[:4], blocks)
    waits = begin(npatch, sources, targets, wide, units, count, index, sems)
    rows, side = pay.shape[1:]
    me = lax.axis_index("patch")
    base = base_of(npatch, me)
    waits[0].wait()

    def put(k, carry):
        place[orders[me, k]] = k - 2
        return carry

    lax.fori_loop(0, npatch, put, 0)
    for j in range(2):
        k = place[lax.rem(base + 3 * j, npatch)]
        waits.append(pltpu.make_async_copy(own.at[j], pay.at[k, PAD : PAD + side], sems.at[len(sources) + 1 + j]))
        waits[-1].start()

    def copies(k):
        result = []
        for j in range(2):
            begin, end = cuts(rows)[j : j + 2]
            if k % 2:
                out = outs[len(turns) + k - 1 + j]
            else:
                turn = sent[k // 2 + 1, j]
                out = outs[turn].at[begin:end] if len(turns[turn]) == 2 else outs[turn]
            result.append(pltpu.make_async_copy(pay.at[k, begin:end], out, sends.at[2 * k + j]))
        return result

    def send(q):
        mine = place[lax.rem(base + q, npatch)]
        add_halos(mine, lax.rem(q + npatch - 1, npatch), q, lax.rem(q + 1, npatch), pay, edges, digits)
        for k in range(npatch - 2):

            @pl.when(mine == k)
            def _():
                for copy in copies(k):
                    copy.start()

    for copy in waits[1:]:
        copy.wait()

    def match(q):
        p = lax.rem(base + q, npatch)
        match_patch(p, q, place[p], slot, units, index, lambda n, r: blocks[n], taps, acc, pay, edges, digits)

    def pair(i, carry):
        match(4 + 2 * i)
        match(5 + 2 * i)
        send(3 + 2 * i)
        send(4 + 2 * i)
        return carry

    lax.fori_loop(0, npatch // 2 - 2, pair, 0)
    send(npatch - 1)
    send(0)
    for k in range(npatch - 2):
        for copy in copies(k):
            copy.wait()


def match_blocks(dest, slot, weights, orders, blocks, taps):
    npatch, number = orders.shape[0], blocks.shape[0]
    edge = blocks.shape[-1]
    side = TH * edge
    rows = side + 2 * PAD
    hbm = pl.BlockSpec(memory_space=pltpu.HBM)
    part = [jax.ShapeDtypeStruct((end - begin, side), jnp.bfloat16) for begin, end in zip(cuts(rows), cuts(rows)[1:])]
    whole = jax.ShapeDtypeStruct((rows, side), jnp.bfloat16)
    params = pltpu.CompilerParams(vmem_limit_bytes=64 * 1024 * 1024)
    ints = pltpu.SMEM((1, number), jnp.int32)

    def scratch(payloads, patches):
        return [
            pltpu.VMEM((SLOTS, edge, edge), jnp.float32),
            pltpu.VMEM((payloads, rows, side), jnp.bfloat16),
            pltpu.VMEM(blocks.shape, jnp.bfloat16),
            pltpu.VMEM(taps.shape, jnp.bfloat16),
            pltpu.VMEM((1, number), jnp.bfloat16),
            pltpu.VMEM((1, number), jnp.int32),
            pltpu.VMEM((patches, 2, PAD, side), jnp.bfloat16),
            pltpu.VMEM((patches, 8, 128), jnp.float32),
            ints,
            ints,
            ints,
        ]

    count = pltpu.SMEM((npatch,), jnp.int32)
    index = pltpu.SMEM((npatch * CAP,), jnp.int32)
    s_a, k_a, both, own, edges, digits = pl.pallas_call(
        lambda *refs: first_kernel(npatch, *refs),
        out_shape=[part[0]] * 2
        + [
            jax.ShapeDtypeStruct((2 * part[1].shape[0], side), jnp.bfloat16),
            jax.ShapeDtypeStruct((2, side, side), jnp.bfloat16),
            jax.ShapeDtypeStruct((4, 2, PAD, side), jnp.bfloat16),
            jax.ShapeDtypeStruct((4, 8, 128), jnp.float32),
        ],
        in_specs=[hbm] * 5,
        out_specs=[hbm] * 6,
        scratch_shapes=[
            *scratch(4, 4),
            count,
            index,
            pltpu.SemaphoreType.DMA((6,)),
            pltpu.SemaphoreType.DMA((8,)),
        ],
        compiler_params=params,
        name="match_first",
    )(dest, slot, weights, blocks, taps)
    turns = make_turns(npatch // 2)
    outs = pl.pallas_call(
        lambda *refs: rest_kernel(npatch, *refs),
        out_shape=[whole if len(turn) == 2 else part[turn[0][1]] for turn in turns[1:]] + part * (npatch // 2 - 1),
        in_specs=[hbm] * 9,
        out_specs=[hbm] * (len(turns) - 1 + npatch - 2),
        scratch_shapes=[
            *scratch(npatch - 2, npatch),
            pltpu.SMEM(orders.shape, jnp.int32),
            count,
            index,
            pltpu.SMEM((npatch,), jnp.int32),
            pltpu.SemaphoreType.DMA((11,)),
            pltpu.SemaphoreType.DMA((2 * (npatch - 2),)),
        ],
        compiler_params=params,
        cost_estimate=pl.CostEstimate(flops=2_000_000_000, bytes_accessed=8_000_000, transcendentals=0),
        name="match_rest",
    )(dest, slot, weights, blocks, taps, jnp.asarray(orders), own, edges, digits)
    sends = [s_a] + list(outs[: len(turns) - 1])
    kept = outs[len(turns) - 1 :]
    return sends, [(k_a, None)] + [(kept[2 * k], kept[2 * k + 1]) for k in range(npatch // 2 - 1)], both


def split(value):
    high = value.astype(jnp.bfloat16)
    return high, (value - high.astype(jnp.float32)).astype(jnp.bfloat16)


def dot3(ah, al, bh, bl, dims):
    def one(a, b):
        return lax.dot_general(a, b, (dims, ((), ())), preferred_element_type=jnp.float32)

    return one(ah, bh) + (one(ah, bl) + one(al, bh))


def chi_rows(place, rowh, rowl, ch, cl, noise):
    rows = pl.ds(pl.multiple_of(place * 128, 128), 128)
    row_pass = dot3(rowh[rows, :], rowl[rows, :], ch, cl, ((1,), (1,)))
    return row_pass * row_pass * (1.0 / noise[0])


def total(x0, x1, x2, x3):
    f32 = jnp.float32
    return x0[...].astype(f32) + x1[...].astype(f32) + (x2[...].astype(f32) + x3[...].astype(f32))


def column_pass(colh, coll, padded):
    high, low = split(padded)
    return split(dot3(colh[...], coll[...], high, low, ((1,), (0,))))


def tail_left(a0, a1, a2, a3, noise, band, colh, coll, rowh, rowl, normed, seam, factor, give, stay):
    f32 = jnp.float32
    rows, side = a0.shape
    edge = side // TH
    left = total(a0, a1, a2, a3)
    lane = lax.broadcasted_iota(jnp.int32, (1, side), 1)
    power = lax.shift_left(jnp.ones((1, side), jnp.int32), lane % DIGITS).astype(f32) * (1.0 / UNIT)
    value = left[0:1, :] * power

    def scale(group, s):
        here = (lane >= group * 128 + s * DIGITS) & (lane < group * 128 + (s + 1) * DIGITS)
        weight_sum = jnp.sum(jnp.where(here, value, 0.0), axis=1, keepdims=True)
        return jnp.broadcast_to(1.0 / jnp.maximum(weight_sum, 1.0), (1, edge))

    def factors(group, column):
        return jnp.concatenate([scale(group, r * TW + column) for r in range(TH)], axis=1)

    right = factors(0, 1)
    left = jnp.concatenate(
        [left[:PAD] * factors(1, TW - 1), left[PAD : PAD + edge] * factors(0, 0), left[PAD + edge :] * right], axis=0
    )
    normed[...] = left[PAD : PAD + edge]
    seam[...] = left[edge:]
    factor[0] = jnp.broadcast_to(right, (8, side))
    factor[1] = jnp.broadcast_to(factors(2, 0), (8, side))
    ch, cl = column_pass(colh, coll, left)
    for j, place in enumerate((band[0], band[0] ^ 2)):
        give[j] = chi_rows(place ^ 1, rowh, rowl, ch, cl, noise)
        stay[j] = chi_rows(place, rowh, rowl, ch, cl, noise)


def tail_right(
    b0, b1, b2, b3, seam, factor, give_left, stay_left, noise, band, colh, coll, rowh, rowl, normed, give, stay
):
    rows, side = b0.shape
    edge = side // TH
    right = total(b0, b1, b2, b3)
    inner = edge - PAD
    right = jnp.concatenate([seam[...], right[:inner] * factor[0, 0:1], right[inner:] * factor[1, 0:1]], axis=0)
    normed[...] = right[PAD : PAD + edge]
    ch, cl = column_pass(colh, coll, right)
    for j, place in enumerate((band[0], band[0] ^ 2)):
        give[j, :, edge:] = chi_rows(place ^ 1, rowh, rowl, ch, cl, noise).astype(give.dtype)
        stay[j, :, edge:] = chi_rows(place, rowh, rowl, ch, cl, noise)
        give[j, :, :edge] = give_left[j].astype(give.dtype)
        stay[j, :, :edge] = stay_left[j]


def tail_image(left, right, image):
    edge = left.shape[0]
    image[:, :edge] = left[...].T
    image[:, edge:] = right[...].T


def tables_kernel(det, colh, coll, rowh, rowl):
    for high, low, start in ((colh, coll, DR - PAD), (rowh, rowl, DR)):
        offsets = (
            lax.broadcasted_iota(jnp.int32, high.shape, 1)
            - lax.broadcasted_iota(jnp.int32, high.shape, 0)
            + start
        )
        table = jnp.zeros(high.shape, jnp.float32)
        for tap in range(det.shape[1]):
            table = jnp.where(offsets == tap, det[0, tap], table)
        high[...], low[...] = split(table)


def filter_tables(det, rows, side):
    return pl.pallas_call(
        tables_kernel,
        out_shape=[jax.ShapeDtypeStruct(s, jnp.bfloat16) for s in [(side // TW, rows)] * 2 + [(side, side)] * 2],
        in_specs=[pl.BlockSpec(memory_space=pltpu.SMEM)],
        out_specs=[pl.BlockSpec(memory_space=pltpu.VMEM)] * 4,
        compiler_params=pltpu.CompilerParams(vmem_limit_bytes=40 * 1024 * 1024),
        cost_estimate=pl.CostEstimate(flops=20_000_000, bytes_accessed=2_000_000, transcendentals=0),
        name="tables",
    )(det)


def finish(left, right, noise, det):
    rows, side = left[0].shape
    f32, bf16 = jnp.float32, jnp.bfloat16
    colh, coll, rowh, rowl = filter_tables(det, rows, side)
    band = lax.axis_index("band")
    where = band.reshape(1).astype(jnp.int32)
    smem = pl.BlockSpec(memory_space=pltpu.SMEM)
    vmem = pl.BlockSpec(memory_space=pltpu.VMEM)
    params = pltpu.CompilerParams(vmem_limit_bytes=40 * 1024 * 1024)
    quarters = jax.ShapeDtypeStruct((2, side // 4, side // TW), f32)
    tile = jax.ShapeDtypeStruct((side // TW, side), f32)
    tables = (colh, coll, rowh, rowl)

    normed_left, seam, factor, give, stay = pl.pallas_call(
        tail_left,
        out_shape=[
            tile,
            jax.ShapeDtypeStruct((2 * PAD, side), f32),
            jax.ShapeDtypeStruct((2, 8, side), f32),
            quarters,
            quarters,
        ],
        in_specs=[vmem] * 4 + [smem] * 2 + [vmem] * 4,
        out_specs=[vmem] * 5,
        compiler_params=params,
        cost_estimate=pl.CostEstimate(flops=500_000_000, bytes_accessed=4_000_000, transcendentals=0),
        name="tail_left",
    )(*left, noise, where, *tables)
    normed_right, give, stay = pl.pallas_call(
        tail_right,
        out_shape=[
            tile,
            jax.ShapeDtypeStruct((2, side // 4, side), bf16),
            jax.ShapeDtypeStruct((2, side // 4, side), f32),
        ],
        in_specs=[vmem] * 8 + [smem] * 2 + [vmem] * 4,
        out_specs=[vmem] * 3,
        compiler_params=params,
        name="tail_right",
    )(*right, seam, factor, give, stay, noise, where, *tables)
    pair = stay + lax.ppermute(give, "band", [(i, i ^ 1) for i in range(4)]).astype(f32)
    beyond = lax.ppermute(pair[1].astype(bf16), "band", [(i, i ^ 2) for i in range(4)])
    normed_right, _ = lax.optimization_barrier((normed_right, pair))
    image = pl.pallas_call(
        tail_image,
        out_shape=jax.ShapeDtypeStruct((side, side), f32),
        in_specs=[vmem] * 2,
        out_specs=vmem,
        compiler_params=params,
        cost_estimate=pl.CostEstimate(flops=0, bytes_accessed=2_000_000, transcendentals=0),
        name="tail_image",
    )(normed_left, normed_right)
    return image, pair[0] + beyond.astype(f32)


def either(flags):
    result = flags[0]
    for flag in flags[1:]:
        result = result | flag
    return result


def local(blocks, dest_patch, dest_slot, weights, psf_taps, det_taps, noise_var):
    f32, bf16 = jnp.float32, jnp.bfloat16
    npatch = lax.axis_size("patch")
    outer = npatch // 2
    me = lax.axis_index("patch")
    z = me // 2
    table = dest_table(outer)
    where_is = np.argsort(table, axis=1)
    order = np.zeros((npatch, npatch), np.int32)
    for i in range(npatch):
        for s in range(outer):
            order[i, 2 * s] = table[i // 2, s] * 2 + 1 - i % 2
            order[i, 2 * s + 1] = table[i // 2, s] * 2 + i % 2
    sends, kept, both = match_blocks(dest_patch, dest_slot, weights, order, blocks[0], psf_taps[0])
    last = outer - 1
    nband = lax.axis_size("band")
    across = [(i, i ^ 1) for i in range(npatch)]
    even = [(i, i ^ 2) for i in range(npatch)]
    odd = []
    for i in range(npatch):
        q = i // 2
        to = q + 1 if q % 2 else q - 1
        for j in range(nband):
            if 0 <= to < outer:
                odd.append((i * nband + j, (2 * to + i % 2) * nband + j))
            else:
                odd.append((i * nband + j, i * nband + (j ^ 1)))
    ends, beside_ends = (0, last), (1, last - 1)

    def place_in(places):
        return either([z == q for q in places])

    def only(places, value):
        return jnp.where(place_in(places), value.astype(f32), 0.0)

    half = both.shape[0] // 2
    with jax.named_scope("even_step_0_right"):
        direct = lax.ppermute(both, "patch", even)
    came = {}
    got = []

    def across_y(send):
        i = len(got)
        if i in (1, 2):
            send, _ = lax.optimization_barrier((send, got[0]))
        if i > 3:
            send, _, _ = lax.optimization_barrier((send, got[i - 2], got[i - 3]))
        with jax.named_scope(f"across_turn_{i}_of"):
            got.append(lax.ppermute(send, "patch", across))

    turns = make_turns(outer)
    for parts, send in zip(turns[:-1], sends, strict=False):
        if len(got) == 3:
            paired = both[:half].astype(f32) + only(beside_ends, direct[:half])
            send = jnp.where(place_in(ends), send.astype(f32), paired).astype(bf16)
        across_y(send)
        for part in parts:
            begin, end = cuts(got[-1].shape[0])[part[1] :][:2]
            came[part] = got[-1][begin:end] if len(parts) == 2 else got[-1]

    def combined(s, c):
        if (s, c) == (0, 1):
            mine = both[half:].astype(f32) + only(beside_ends, direct[half:])
            return mine + came[last - 1, 1].astype(f32)
        if (s, c) == (last - 1, 1):
            return kept[s][c].astype(f32) + only(ends, came[s, c])
        mine, other = kept[s][c], came[s, c]
        if s == 0:
            other, _ = lax.optimization_barrier((other, sends[1]))
        return mine.astype(f32) + other.astype(f32)

    def chosen(places, c):
        values = sorted(set(places.values()))
        result = combined(values[-1], c)
        for v in values[:-1]:
            result = jnp.where(either([z == q for q, s in places.items() if s == v]), combined(v, c), result)
        return result

    def step(t, parity, c):
        places = {}
        for q in range(outer):
            rising = q % 2 == parity
            hops = q if rising else last - q
            d = last - t + q if rising else t - hops
            if hops <= t and 0 <= d < outer and d != q:
                places[q] = int(where_is[q][d])
        return chosen(places, c)

    def masked(value):
        return jnp.where(place_in(ends), 0.0, value.astype(f32))

    evens, odds, send_even = [None, None], [None, None], [None, None]
    for t in range(last):
        for c in range(2):
            side = "left" if c == 0 else "right"
            send = None if (t, c) == (0, 1) else step(t, 0, c)
            if t > 1:
                send = send + masked(odds[c])
            send_odd = step(t, 1, c) if t else None
            if (t, c) == (2, 1):
                send, _ = lax.optimization_barrier((send, came[last, 0]))
            if t and (t, c) != (1, 1):
                send_odd = send_odd + evens[c].astype(f32)
            if (t, c) == (1, 1):
                passing, _ = lax.optimization_barrier((sends[3], got[1]))
                send = jnp.where(place_in(ends), send, passing.astype(f32))
            if send is not None:
                with jax.named_scope(f"even_step_{t}_{side}"):
                    send_even[c] = send.astype(bf16)
                    evens[c] = lax.ppermute(send_even[c], "patch", even)
            if (t, c) == (1, 1):
                passed = jnp.where(place_in(beside_ends), 0.0, evens[c].astype(f32))
                across_y((sends[-1].astype(f32) + passed).astype(bf16))
                came[last, 1] = got[-1]
            if (t, c) == (1, 1):
                det_taps, _ = lax.optimization_barrier((det_taps, evens[c]))
            if (t, c) == (2, 1):
                send_odd, _ = lax.optimization_barrier((send_odd.astype(bf16), send_even[0]))
            if t:
                with jax.named_scope(f"odd_step_{t}_{side}"):
                    odds[c] = lax.ppermute(send_odd.astype(bf16), ("patch", "band"), odd)
    for c in range(2):
        odds[c] = masked(odds[c]).astype(bf16)
    parts = [(kept[last][c], came[last, c], evens[c], odds[c]) for c in range(2)]
    image, chi = finish(*parts, noise_var, det_taps)
    return image[None], chi


def solution(mesh):
    in_specs = (
        P("band", "patch", None, None),
        P("band", "patch"),
        P("band", "patch"),
        P("band", "patch"),
        P("band", "patch", None, None),
        P("band", None),
        P("band"),
    )
    out_specs = (P("band", None, "patch"), P("band", "patch"))
    return jax.shard_map(local, mesh=mesh, in_specs=in_specs, out_specs=out_specs, check_vma=False)
```

```python
import jax
import jax.numpy as jnp
import numpy as np
from jax import lax
from jax.experimental import pallas as pl
from jax.experimental.pallas import tpu as pltpu
from jax.sharding import PartitionSpec as P

TH = 2
TW = 2
DR = 12
CAP = 4
SLOTS = 4
PAD = 16
DIGITS = 16
UNIT = 512


def cuts(rows):
    return (0, rows // 2 + PAD, rows)


def dest_table(outer):
    table = np.zeros((outer, outer), np.int32)
    for z in range(outer):
        def due(d):
            if d > z:
                return (outer - 1 + z - d, d == z ^ 1)
            if d < z:
                return (outer - 1 - z + d, d == z ^ 1)
            return (outer, 0)

        table[z] = sorted(range(outer), key=due)
    return table


def toeplitz(row):
    half = row.shape[1] // 2
    wide = jnp.broadcast_to(row, (half, 2 * half))
    skew = pltpu.roll(wide, 0, 1, stride=1, stride_axis=0)
    diag = skew[:, :half]
    off = skew[:, half:]
    i = lax.broadcasted_iota(jnp.int32, (half, half), 0)
    j = lax.broadcasted_iota(jnp.int32, (half, half), 1)
    upper = jnp.where(j < i, off, 0.0)
    lower = jnp.where(j > i, off, 0.0)
    top = jnp.concatenate([diag, upper], axis=1)
    bottom = jnp.concatenate([lower, diag], axis=1)
    return jnp.concatenate([top, bottom], axis=0).astype(jnp.bfloat16)


def make_lists(npatch, dest, count, index):
    def clear(p, carry):
        count[p] = 0
        for r in range(CAP):
            index[p * CAP + r] = -1
        return carry

    lax.fori_loop(0, npatch, clear, 0)

    def place(n, carry):
        p = dest[0, n]
        r = count[p]
        count[p] = r + 1
        index[p * CAP + r] = n
        return carry

    lax.fori_loop(0, dest.shape[1], place, 0)


def match_patch(p, q, k, slot, units, index, block, taps, acc, pay, edges, digits):
    edge = acc.shape[-1]
    ntaps = taps.shape[-1]
    side = TH * edge
    lane = lax.broadcasted_iota(jnp.int32, (8, 128), 1)
    acc[...] = jnp.zeros(acc.shape, acc.dtype)
    row = jnp.zeros((8, 128), jnp.float32)
    for r in range(CAP):
        found = index[p * CAP + r]
        n = jnp.maximum(found, 0)
        s = slot[0, n]
        unit = jnp.where(found >= 0, units[0, n], 0)
        w = unit.astype(jnp.float32) * (1.0 / UNIT)
        tap = taps[n].astype(jnp.float32)
        tap = jnp.concatenate([tap, jnp.zeros((2, edge - ntaps), jnp.float32)], axis=1)
        tap = pltpu.roll(tap, edge - ntaps // 2, 1)
        col = toeplitz(tap[0:1])
        half = jnp.dot(col, block(n, r), preferred_element_type=jnp.float32).astype(jnp.bfloat16)
        rowm = toeplitz(tap[1:2])
        matched = lax.dot_general(
            rowm, half, (((1,), (1,)), ((), ())), preferred_element_type=jnp.float32
        ).astype(jnp.bfloat16)
        acc[s] = acc[s] + w * matched.astype(jnp.float32)
        bit = lax.shift_right_logical(jnp.full((8, 128), unit), lane % DIGITS) & 1
        row = row + jnp.where(lane // DIGITS == s, bit, 0).astype(jnp.float32)
    digits[q] = row
    for s in range(SLOTS):
        top = (s % TW) * edge
        left = (s // TW) * edge
        pay[k, PAD + top : PAD + top + edge, left : left + edge] = acc[s].astype(jnp.bfloat16)
    edges[q, 0] = pay[k, PAD : 2 * PAD, :]
    edges[q, 1] = pay[k, side : side + PAD, :]


def add_halos(k, before, q, after, pay, edges, digits):
    rows, side = pay.shape[1:]
    first = lax.broadcasted_iota(jnp.int32, (PAD, side), 0) == 0
    blank = jnp.zeros((8, side - 3 * 128), jnp.float32)
    row = jnp.concatenate([digits[q], digits[before], digits[after], blank], axis=1)
    row = jnp.concatenate([row, row], axis=0)
    pay[k, :PAD, :] = jnp.where(first, row, edges[before, 1].astype(jnp.float32)).astype(jnp.bfloat16)
    pay[k, rows - PAD :, :] = edges[after, 0]


def begin(npatch, sources, targets, wide, units, count, index, sems):
    fetched = [pltpu.make_async_copy(x, y, sems.at[i]) for i, (x, y) in enumerate(zip(sources, targets, strict=True))]
    for copy in fetched:
        copy.start()
    dest, weights = targets[:2]
    fetched[1].wait()
    wide[...] = (weights[...].astype(jnp.float32) * UNIT).astype(jnp.int32)
    convert = pltpu.make_async_copy(wide, units, sems.at[len(fetched)])
    convert.start()
    fetched[0].wait()
    make_lists(npatch, dest, count, index)
    return [*fetched[2:], convert]


def base_of(npatch, me):
    return jnp.where(2 * (me // 2) < npatch // 2, npatch - 3, npatch - 1)


def first_kernel(
    npatch, dest_in, slot_in, weights_in, blocks_in, taps_in, s_a, k_a, both, own, edges_out, digits_out,
    acc, pay, blocks, taps, weights, wide, edges, digits, dest, slot, units, count, index, sems, sends,
):
    sources = (dest_in, weights_in, slot_in, taps_in, blocks_in)
    waits = begin(npatch, sources, (dest, weights, slot, taps, blocks), wide, units, count, index, sems)
    me = lax.axis_index("patch")
    base = base_of(npatch, me)
    for copy in waits:
        copy.wait()
    rows, side = pay.shape[1:]
    copies = []

    def send(source, out):
        copies.append(pltpu.make_async_copy(source, out, sends.at[len(copies)]))
        copies[-1].start()

    def either_way(first_out, second_out, q, part):
        source = pay.at[q, cuts(rows)[part] : cuts(rows)[part + 1]]
        copy = [pltpu.make_async_copy(source, out, sends.at[len(copies)]) for out in (first_out, second_out)]
        copies.append(copy[0])
        goes = lax.rem(me, 2) == 2 - q
        pl.when(goes)(copy[0].start)
        pl.when(jnp.logical_not(goes))(copy[1].start)

    def match(q):
        p = lax.rem(base + q, npatch)
        match_patch(p, q, q, slot, units, index, lambda n, r: blocks[n], taps, acc, pay, edges, digits)

    match(0)
    match(1)
    send(pay.at[0, PAD : PAD + side], own.at[0])
    match(2)
    match(3)
    height = both.shape[0] // 2
    for q in (1, 2):
        add_halos(q, q - 1, q, q + 1, pay, edges, digits)
        either_way(s_a, k_a, q, 0)
        either_way(both.at[:height], both.at[height:], q, 1)
    send(pay.at[3, PAD : PAD + side], own.at[1])
    send(edges, edges_out)
    send(digits, digits_out)
    for copy in copies:
        copy.wait()


def make_turns(outer):
    last = outer - 1
    turns = [[(0, 0)], [(1, 0)], [(1, 1)], [(last - 1, 1)]]
    turns += [[(s, 0), (s, 1)] for s in range(2, last - 1)]
    return turns + [[(last - 1, 0)], [(last, 0)], [(last, 1)]]


def rest_kernel(
    npatch, dest_in, slot_in, weights_in, blocks_in, taps_in, orders_in, own, edges_in, digits_in, *rest
):
    turns = make_turns(npatch // 2)[1:]
    sent = {part: turn for turn, parts in enumerate(turns) for part in parts}
    number = len(turns) + npatch - 2
    outs = rest[:number]
    (
        acc, pay, blocks, taps, weights, wide, edges, digits,
        dest, slot, units, orders, count, index, place, sems, sends,
    ) = rest[number:]
    sources = (dest_in, weights_in, orders_in, slot_in, taps_in, edges_in, digits_in, blocks_in)
    targets = (dest, weights, orders, slot, taps, edges.at[:4], digits.at[:4], blocks)
    waits = begin(npatch, sources, targets, wide, units, count, index, sems)
    rows, side = pay.shape[1:]
    me = lax.axis_index("patch")
    base = base_of(npatch, me)
    waits[0].wait()

    def put(k, carry):
        place[orders[me, k]] = k - 2
        return carry

    lax.fori_loop(0, npatch, put, 0)
    for j in range(2):
        k = place[lax.rem(base + 3 * j, npatch)]
        waits.append(pltpu.make_async_copy(own.at[j], pay.at[k, PAD : PAD + side], sems.at[len(sources) + 1 + j]))
        waits[-1].start()

    def copies(k):
        result = []
        for j in range(2):
            begin, end = cuts(rows)[j : j + 2]
            if k % 2:
                out = outs[len(turns) + k - 1 + j]
            else:
                turn = sent[k // 2 + 1, j]
                out = outs[turn].at[begin:end] if len(turns[turn]) == 2 else outs[turn]
            result.append(pltpu.make_async_copy(pay.at[k, begin:end], out, sends.at[2 * k + j]))
        return result

    def send(q):
        mine = place[lax.rem(base + q, npatch)]
        add_halos(mine, lax.rem(q + npatch - 1, npatch), q, lax.rem(q + 1, npatch), pay, edges, digits)
        for k in range(npatch - 2):

            @pl.when(mine == k)
            def _():
                for copy in copies(k):
                    copy.start()

    for copy in waits[1:]:
        copy.wait()

    def match(q):
        p = lax.rem(base + q, npatch)
        match_patch(p, q, place[p], slot, units, index, lambda n, r: blocks[n], taps, acc, pay, edges, digits)

    def pair(i, carry):
        match(4 + 2 * i)
        match(5 + 2 * i)
        send(3 + 2 * i)
        send(4 + 2 * i)
        return carry

    lax.fori_loop(0, npatch // 2 - 2, pair, 0)
    send(npatch - 1)
    send(0)
    for k in range(npatch - 2):
        for copy in copies(k):
            copy.wait()


def match_blocks(dest, slot, weights, orders, blocks, taps):
    npatch, number = orders.shape[0], blocks.shape[0]
    edge = blocks.shape[-1]
    side = TH * edge
    rows = side + 2 * PAD
    hbm = pl.BlockSpec(memory_space=pltpu.HBM)
    part = [jax.ShapeDtypeStruct((end - begin, side), jnp.bfloat16) for begin, end in zip(cuts(rows), cuts(rows)[1:])]
    whole = jax.ShapeDtypeStruct((rows, side), jnp.bfloat16)
    params = pltpu.CompilerParams(vmem_limit_bytes=64 * 1024 * 1024)
    ints = pltpu.SMEM((1, number), jnp.int32)

    def scratch(payloads, patches):
        return [
            pltpu.VMEM((SLOTS, edge, edge), jnp.float32),
            pltpu.VMEM((payloads, rows, side), jnp.bfloat16),
            pltpu.VMEM(blocks.shape, jnp.bfloat16),
            pltpu.VMEM(taps.shape, jnp.bfloat16),
            pltpu.VMEM((1, number), jnp.bfloat16),
            pltpu.VMEM((1, number), jnp.int32),
            pltpu.VMEM((patches, 2, PAD, side), jnp.bfloat16),
            pltpu.VMEM((patches, 8, 128), jnp.float32),
            ints,
            ints,
            ints,
        ]

    count = pltpu.SMEM((npatch,), jnp.int32)
    index = pltpu.SMEM((npatch * CAP,), jnp.int32)
    s_a, k_a, both, own, edges, digits = pl.pallas_call(
        lambda *refs: first_kernel(npatch, *refs),
        out_shape=[part[0]] * 2
        + [
            jax.ShapeDtypeStruct((2 * part[1].shape[0], side), jnp.bfloat16),
            jax.ShapeDtypeStruct((2, side, side), jnp.bfloat16),
            jax.ShapeDtypeStruct((4, 2, PAD, side), jnp.bfloat16),
            jax.ShapeDtypeStruct((4, 8, 128), jnp.float32),
        ],
        in_specs=[hbm] * 5,
        out_specs=[hbm] * 6,
        scratch_shapes=[
            *scratch(4, 4),
            count,
            index,
            pltpu.SemaphoreType.DMA((6,)),
            pltpu.SemaphoreType.DMA((8,)),
        ],
        compiler_params=params,
        name="match_first",
    )(dest, slot, weights, blocks, taps)
    turns = make_turns(npatch // 2)
    outs = pl.pallas_call(
        lambda *refs: rest_kernel(npatch, *refs),
        out_shape=[whole if len(turn) == 2 else part[turn[0][1]] for turn in turns[1:]] + part * (npatch // 2 - 1),
        in_specs=[hbm] * 9,
        out_specs=[hbm] * (len(turns) - 1 + npatch - 2),
        scratch_shapes=[
            *scratch(npatch - 2, npatch),
            pltpu.SMEM(orders.shape, jnp.int32),
            count,
            index,
            pltpu.SMEM((npatch,), jnp.int32),
            pltpu.SemaphoreType.DMA((11,)),
            pltpu.SemaphoreType.DMA((2 * (npatch - 2),)),
        ],
        compiler_params=params,
        cost_estimate=pl.CostEstimate(flops=2_000_000_000, bytes_accessed=8_000_000, transcendentals=0),
        name="match_rest",
    )(dest, slot, weights, blocks, taps, jnp.asarray(orders), own, edges, digits)
    sends = [s_a] + list(outs[: len(turns) - 1])
    kept = outs[len(turns) - 1 :]
    return sends, [(k_a, None)] + [(kept[2 * k], kept[2 * k + 1]) for k in range(npatch // 2 - 1)], both


def split(value):
    high = value.astype(jnp.bfloat16)
    return high, (value - high.astype(jnp.float32)).astype(jnp.bfloat16)


def dot3(ah, al, bh, bl, dims):
    def one(a, b):
        return lax.dot_general(a, b, (dims, ((), ())), preferred_element_type=jnp.float32)

    return one(ah, bh) + (one(ah, bl) + one(al, bh))


def chi_rows(place, rowh, rowl, ch, cl, noise):
    rows = pl.ds(pl.multiple_of(place * 128, 128), 128)
    row_pass = dot3(rowh[rows, :], rowl[rows, :], ch, cl, ((1,), (1,)))
    return row_pass * row_pass * (1.0 / noise[0])


def total(x0, x1, x2, x3):
    f32 = jnp.float32
    return x0[...].astype(f32) + x1[...].astype(f32) + (x2[...].astype(f32) + x3[...].astype(f32))


def column_pass(colh, coll, padded):
    high, low = split(padded)
    return split(dot3(colh[...], coll[...], high, low, ((1,), (0,))))


def tail_left(a0, a1, a2, a3, noise, band, colh, coll, rowh, rowl, normed, seam, factor, give, stay):
    f32 = jnp.float32
    rows, side = a0.shape
    edge = side // TH
    left = total(a0, a1, a2, a3)
    lane = lax.broadcasted_iota(jnp.int32, (1, side), 1)
    power = lax.shift_left(jnp.ones((1, side), jnp.int32), lane % DIGITS).astype(f32) * (1.0 / UNIT)
    value = left[0:1, :] * power

    def scale(group, s):
        here = (lane >= group * 128 + s * DIGITS) & (lane < group * 128 + (s + 1) * DIGITS)
        weight_sum = jnp.sum(jnp.where(here, value, 0.0), axis=1, keepdims=True)
        return jnp.broadcast_to(1.0 / jnp.maximum(weight_sum, 1.0), (1, edge))

    def factors(group, column):
        return jnp.concatenate([scale(group, r * TW + column) for r in range(TH)], axis=1)

    right = factors(0, 1)
    left = jnp.concatenate(
        [left[:PAD] * factors(1, TW - 1), left[PAD : PAD + edge] * factors(0, 0), left[PAD + edge :] * right], axis=0
    )
    normed[...] = left[PAD : PAD + edge]
    seam[...] = left[edge:]
    factor[0] = jnp.broadcast_to(right, (8, side))
    factor[1] = jnp.broadcast_to(factors(2, 0), (8, side))
    ch, cl = column_pass(colh, coll, left)
    for j, place in enumerate((band[0], band[0] ^ 2)):
        give[j] = chi_rows(place ^ 1, rowh, rowl, ch, cl, noise)
        stay[j] = chi_rows(place, rowh, rowl, ch, cl, noise)


def tail_right(
    b0, b1, b2, b3, seam, factor, give_left, stay_left, noise, band, colh, coll, rowh, rowl, normed, give, stay
):
    rows, side = b0.shape
    edge = side // TH
    right = total(b0, b1, b2, b3)
    inner = edge - PAD
    right = jnp.concatenate([seam[...], right[:inner] * factor[0, 0:1], right[inner:] * factor[1, 0:1]], axis=0)
    normed[...] = right[PAD : PAD + edge]
    ch, cl = column_pass(colh, coll, right)
    for j, place in enumerate((band[0], band[0] ^ 2)):
        give[j, :, edge:] = chi_rows(place ^ 1, rowh, rowl, ch, cl, noise).astype(give.dtype)
        stay[j, :, edge:] = chi_rows(place, rowh, rowl, ch, cl, noise)
        give[j, :, :edge] = give_left[j].astype(give.dtype)
        stay[j, :, :edge] = stay_left[j]


def tail_image(left, right, image):
    edge = left.shape[0]
    image[:, :edge] = left[...].T
    image[:, edge:] = right[...].T


def tables_kernel(det, colh, coll, rowh, rowl):
    for high, low, start in ((colh, coll, DR - PAD), (rowh, rowl, DR)):
        offsets = (
            lax.broadcasted_iota(jnp.int32, high.shape, 1)
            - lax.broadcasted_iota(jnp.int32, high.shape, 0)
            + start
        )
        table = jnp.zeros(high.shape, jnp.float32)
        for tap in range(det.shape[1]):
            table = jnp.where(offsets == tap, det[0, tap], table)
        high[...], low[...] = split(table)


def filter_tables(det, rows, side):
    return pl.pallas_call(
        tables_kernel,
        out_shape=[jax.ShapeDtypeStruct(s, jnp.bfloat16) for s in [(side // TW, rows)] * 2 + [(side, side)] * 2],
        in_specs=[pl.BlockSpec(memory_space=pltpu.SMEM)],
        out_specs=[pl.BlockSpec(memory_space=pltpu.VMEM)] * 4,
        compiler_params=pltpu.CompilerParams(vmem_limit_bytes=40 * 1024 * 1024),
        cost_estimate=pl.CostEstimate(flops=20_000_000, bytes_accessed=2_000_000, transcendentals=0),
        name="tables",
    )(det)


def finish(left, right, noise, det):
    rows, side = left[0].shape
    f32, bf16 = jnp.float32, jnp.bfloat16
    colh, coll, rowh, rowl = filter_tables(det, rows, side)
    band = lax.axis_index("band")
    where = band.reshape(1).astype(jnp.int32)
    smem = pl.BlockSpec(memory_space=pltpu.SMEM)
    vmem = pl.BlockSpec(memory_space=pltpu.VMEM)
    params = pltpu.CompilerParams(vmem_limit_bytes=40 * 1024 * 1024)
    quarters = jax.ShapeDtypeStruct((2, side // 4, side // TW), f32)
    tile = jax.ShapeDtypeStruct((side // TW, side), f32)
    tables = (colh, coll, rowh, rowl)

    normed_left, seam, factor, give, stay = pl.pallas_call(
        tail_left,
        out_shape=[
            tile,
            jax.ShapeDtypeStruct((2 * PAD, side), f32),
            jax.ShapeDtypeStruct((2, 8, side), f32),
            quarters,
            quarters,
        ],
        in_specs=[vmem] * 4 + [smem] * 2 + [vmem] * 4,
        out_specs=[vmem] * 5,
        compiler_params=params,
        cost_estimate=pl.CostEstimate(flops=500_000_000, bytes_accessed=4_000_000, transcendentals=0),
        name="tail_left",
    )(*left, noise, where, *tables)
    normed_right, give, stay = pl.pallas_call(
        tail_right,
        out_shape=[
            tile,
            jax.ShapeDtypeStruct((2, side // 4, side), bf16),
            jax.ShapeDtypeStruct((2, side // 4, side), f32),
        ],
        in_specs=[vmem] * 8 + [smem] * 2 + [vmem] * 4,
        out_specs=[vmem] * 3,
        compiler_params=params,
        name="tail_right",
    )(*right, seam, factor, give, stay, noise, where, *tables)
    pair = stay + lax.ppermute(give, "band", [(i, i ^ 1) for i in range(4)]).astype(f32)
    beyond = lax.ppermute(pair[1].astype(bf16), "band", [(i, i ^ 2) for i in range(4)])
    normed_right, _ = lax.optimization_barrier((normed_right, pair))
    image = pl.pallas_call(
        tail_image,
        out_shape=jax.ShapeDtypeStruct((side, side), f32),
        in_specs=[vmem] * 2,
        out_specs=vmem,
        compiler_params=params,
        cost_estimate=pl.CostEstimate(flops=0, bytes_accessed=2_000_000, transcendentals=0),
        name="tail_image",
    )(normed_left, normed_right)
    return image, pair[0] + beyond.astype(f32)


def either(flags):
    result = flags[0]
    for flag in flags[1:]:
        result = result | flag
    return result


def local(blocks, dest_patch, dest_slot, weights, psf_taps, det_taps, noise_var):
    f32, bf16 = jnp.float32, jnp.bfloat16
    npatch = lax.axis_size("patch")
    outer = npatch // 2
    me = lax.axis_index("patch")
    z = me // 2
    table = dest_table(outer)
    where_is = np.argsort(table, axis=1)
    order = np.zeros((npatch, npatch), np.int32)
    for i in range(npatch):
        for s in range(outer):
            order[i, 2 * s] = table[i // 2, s] * 2 + 1 - i % 2
            order[i, 2 * s + 1] = table[i // 2, s] * 2 + i % 2
    sends, kept, both = match_blocks(dest_patch, dest_slot, weights, order, blocks[0], psf_taps[0])
    last = outer - 1
    nband = lax.axis_size("band")
    across = [(i, i ^ 1) for i in range(npatch)]
    even = [(i, i ^ 2) for i in range(npatch)]
    odd = []
    for i in range(npatch):
        q = i // 2
        to = q + 1 if q % 2 else q - 1
        for j in range(nband):
            if 0 <= to < outer:
                odd.append((i * nband + j, (2 * to + i % 2) * nband + j))
            else:
                odd.append((i * nband + j, i * nband + (j ^ 1)))
    ends, beside_ends = (0, last), (1, last - 1)

    def place_in(places):
        return either([z == q for q in places])

    def only(places, value):
        return jnp.where(place_in(places), value.astype(f32), 0.0)

    half = both.shape[0] // 2
    with jax.named_scope("even_step_0_right"):
        direct = lax.ppermute(both, "patch", even)
    came = {}
    got = []

    def across_y(send):
        i = len(got)
        if i in (1, 2):
            send, _ = lax.optimization_barrier((send, got[0]))
        if i > 3:
            send, _, _ = lax.optimization_barrier((send, got[i - 2], got[i - 3]))
        with jax.named_scope(f"across_turn_{i}_of"):
            got.append(lax.ppermute(send, "patch", across))

    turns = make_turns(outer)
    for parts, send in zip(turns[:-1], sends, strict=False):
        if len(got) == 3:
            paired = both[:half].astype(f32) + only(beside_ends, direct[:half])
            send = jnp.where(place_in(ends), send.astype(f32), paired).astype(bf16)
        across_y(send)
        for part in parts:
            begin, end = cuts(got[-1].shape[0])[part[1] :][:2]
            came[part] = got[-1][begin:end] if len(parts) == 2 else got[-1]

    def combined(s, c):
        if (s, c) == (0, 1):
            mine = both[half:].astype(f32) + only(beside_ends, direct[half:])
            return mine + came[last - 1, 1].astype(f32)
        if (s, c) == (last - 1, 1):
            return kept[s][c].astype(f32) + only(ends, came[s, c])
        mine, other = kept[s][c], came[s, c]
        if s == 0:
            other, _ = lax.optimization_barrier((other, sends[1]))
        return mine.astype(f32) + other.astype(f32)

    def chosen(places, c):
        values = sorted(set(places.values()))
        result = combined(values[-1], c)
        for v in values[:-1]:
            result = jnp.where(either([z == q for q, s in places.items() if s == v]), combined(v, c), result)
        return result

    def step(t, parity, c):
        places = {}
        for q in range(outer):
            rising = q % 2 == parity
            hops = q if rising else last - q
            d = last - t + q if rising else t - hops
            if hops <= t and 0 <= d < outer and d != q:
                places[q] = int(where_is[q][d])
        return chosen(places, c)

    def masked(value):
        return jnp.where(place_in(ends), 0.0, value.astype(f32))

    evens, odds, send_even = [None, None], [None, None], [None, None]
    for t in range(last):
        for c in range(2):
            side = "left" if c == 0 else "right"
            if (t, c) == (1, 1):
                came[1, 1], *_ = lax.optimization_barrier((came[1, 1], *earlier))
            send = None if (t, c) == (0, 1) else step(t, 0, c)
            if (t, c) == (2, 0):
                odds[0], _ = lax.optimization_barrier((odds[0], sent_odd))
            if t > 1:
                send = send + masked(odds[c])
            if (t, c) == (1, 1):
                ahead = (step(2, 1, 0) + evens[0].astype(f32)).astype(bf16)
                came[last - 1, 1], *_ = lax.optimization_barrier((came[last - 1, 1], ahead, odds[0]))
            send_odd = step(t, 1, c) if t else None
            if (t, c) == (2, 1):
                send, _ = lax.optimization_barrier((send, came[last, 0]))
            if (t, c) == (2, 0):
                send_odd = ahead
            elif t and (t, c) != (1, 1):
                send_odd = send_odd + evens[c].astype(f32)
            if (t, c) == (1, 1):
                passing, _ = lax.optimization_barrier((sends[3], got[1]))
                send = jnp.where(place_in(ends), send, passing.astype(f32))
            if send is not None:
                with jax.named_scope(f"even_step_{t}_{side}"):
                    send_even[c] = send.astype(bf16)
                    evens[c] = lax.ppermute(send_even[c], "patch", even)
            if (t, c) == (1, 1):
                evens[c], *_ = lax.optimization_barrier((evens[c], ahead, odds[0]))
                passed = jnp.where(place_in(beside_ends), 0.0, evens[c].astype(f32))
                final = (sends[-1].astype(f32) + passed).astype(bf16)
            if (t, c) == (1, 1):
                det_taps, _ = lax.optimization_barrier((det_taps, evens[c]))
            if (t, c) == (2, 1):
                send_odd, _ = lax.optimization_barrier((send_odd.astype(bf16), send_even[0]))
            if (t, c) == (1, 0):
                earlier = send_even[0], send_odd.astype(bf16)
            if t:
                sent_odd = send_odd.astype(bf16)
                with jax.named_scope(f"odd_step_{t}_{side}"):
                    odds[c] = lax.ppermute(send_odd.astype(bf16), ("patch", "band"), odd)
            if (t, c) == (2, 1):
                final, _ = lax.optimization_barrier((final, send_even[1]))
                across_y(final)
                came[last, 1] = got[-1]
    odds[1], _ = lax.optimization_barrier((odds[1], evens[0]))
    for c in range(2):
        odds[c] = masked(odds[c]).astype(bf16)
    parts = [(kept[last][c], came[last, c], evens[c], odds[c]) for c in range(2)]
    image, chi = finish(*parts, noise_var, det_taps)
    return image[None], chi


def solution(mesh):
    in_specs = (
        P("band", "patch", None, None),
        P("band", "patch"),
        P("band", "patch"),
        P("band", "patch"),
        P("band", "patch", None, None),
        P("band", None),
        P("band"),
    )
    out_specs = (P("band", None, "patch"), P("band", "patch"))
    return jax.shard_map(local, mesh=mesh, in_specs=in_specs, out_specs=out_specs, check_vma=False)
```

```python
import jax
import jax.numpy as jnp
import numpy as np
from jax import lax
from jax.experimental import pallas as pl
from jax.experimental.pallas import tpu as pltpu
from jax.sharding import PartitionSpec as P

TH = 2
TW = 2
DR = 12
CAP = 4
SLOTS = 4
PAD = 16
DIGITS = 16
UNIT = 512


def cuts(rows):
    return (0, rows // 2 + PAD, rows)


def dest_table(outer):
    table = np.zeros((outer, outer), np.int32)
    for z in range(outer):
        def due(d):
            if d > z:
                return (outer - 1 + z - d, d == z ^ 1)
            if d < z:
                return (outer - 1 - z + d, d == z ^ 1)
            return (outer, 0)

        table[z] = sorted(range(outer), key=due)
    return table


def toeplitz(row):
    half = row.shape[1] // 2
    wide = jnp.broadcast_to(row, (half, 2 * half))
    skew = pltpu.roll(wide, 0, 1, stride=1, stride_axis=0)
    diag = skew[:, :half]
    off = skew[:, half:]
    i = lax.broadcasted_iota(jnp.int32, (half, half), 0)
    j = lax.broadcasted_iota(jnp.int32, (half, half), 1)
    upper = jnp.where(j < i, off, 0.0)
    lower = jnp.where(j > i, off, 0.0)
    top = jnp.concatenate([diag, upper], axis=1)
    bottom = jnp.concatenate([lower, diag], axis=1)
    return jnp.concatenate([top, bottom], axis=0).astype(jnp.bfloat16)


def make_lists(npatch, dest, count, index):
    def clear(p, carry):
        count[p] = 0
        for r in range(CAP):
            index[p * CAP + r] = -1
        return carry

    lax.fori_loop(0, npatch, clear, 0)

    def place(n, carry):
        p = dest[0, n]
        r = count[p]
        count[p] = r + 1
        index[p * CAP + r] = n
        return carry

    lax.fori_loop(0, dest.shape[1], place, 0)


def match_patch(p, q, k, slot, units, index, block, taps, acc, pay, edges, digits):
    edge = acc.shape[-1]
    ntaps = taps.shape[-1]
    side = TH * edge
    lane = lax.broadcasted_iota(jnp.int32, (8, 128), 1)
    acc[...] = jnp.zeros(acc.shape, acc.dtype)
    row = jnp.zeros((8, 128), jnp.float32)
    for r in range(CAP):
        found = index[p * CAP + r]
        n = jnp.maximum(found, 0)
        s = slot[0, n]
        unit = jnp.where(found >= 0, units[0, n], 0)
        w = unit.astype(jnp.float32) * (1.0 / UNIT)
        tap = taps[n].astype(jnp.float32)
        tap = jnp.concatenate([tap, jnp.zeros((2, edge - ntaps), jnp.float32)], axis=1)
        tap = pltpu.roll(tap, edge - ntaps // 2, 1)
        col = toeplitz(tap[0:1])
        half = jnp.dot(col, block(n, r), preferred_element_type=jnp.float32).astype(jnp.bfloat16)
        rowm = toeplitz(tap[1:2])
        matched = lax.dot_general(
            rowm, half, (((1,), (1,)), ((), ())), preferred_element_type=jnp.float32
        ).astype(jnp.bfloat16)
        acc[s] = acc[s] + w * matched.astype(jnp.float32)
        bit = lax.shift_right_logical(jnp.full((8, 128), unit), lane % DIGITS) & 1
        row = row + jnp.where(lane // DIGITS == s, bit, 0).astype(jnp.float32)
    digits[q] = row
    for s in range(SLOTS):
        top = (s % TW) * edge
        left = (s // TW) * edge
        pay[k, PAD + top : PAD + top + edge, left : left + edge] = acc[s].astype(jnp.bfloat16)
    edges[q, 0] = pay[k, PAD : 2 * PAD, :]
    edges[q, 1] = pay[k, side : side + PAD, :]


def add_halos(k, before, q, after, pay, edges, digits):
    rows, side = pay.shape[1:]
    first = lax.broadcasted_iota(jnp.int32, (PAD, side), 0) == 0
    blank = jnp.zeros((8, side - 3 * 128), jnp.float32)
    row = jnp.concatenate([digits[q], digits[before], digits[after], blank], axis=1)
    row = jnp.concatenate([row, row], axis=0)
    pay[k, :PAD, :] = jnp.where(first, row, edges[before, 1].astype(jnp.float32)).astype(jnp.bfloat16)
    pay[k, rows - PAD :, :] = edges[after, 0]


def begin(npatch, sources, targets, wide, units, count, index, sems):
    fetched = [pltpu.make_async_copy(x, y, sems.at[i]) for i, (x, y) in enumerate(zip(sources, targets, strict=True))]
    for copy in fetched:
        copy.start()
    dest, weights = targets[:2]
    fetched[1].wait()
    wide[...] = (weights[...].astype(jnp.float32) * UNIT).astype(jnp.int32)
    convert = pltpu.make_async_copy(wide, units, sems.at[len(fetched)])
    convert.start()
    fetched[0].wait()
    make_lists(npatch, dest, count, index)
    return [*fetched[2:], convert]


def base_of(npatch, me):
    return jnp.where(2 * (me // 2) < npatch // 2, npatch - 3, npatch - 1)


def first_kernel(
    npatch, dest_in, slot_in, weights_in, blocks_in, taps_in, s_a, k_a, both, own, edges_out, digits_out,
    acc, pay, blocks, taps, weights, wide, edges, digits, dest, slot, units, count, index, sems, sends,
):
    sources = (dest_in, weights_in, slot_in, taps_in, blocks_in)
    waits = begin(npatch, sources, (dest, weights, slot, taps, blocks), wide, units, count, index, sems)
    me = lax.axis_index("patch")
    base = base_of(npatch, me)
    for copy in waits:
        copy.wait()
    rows, side = pay.shape[1:]
    copies = []

    def send(source, out):
        copies.append(pltpu.make_async_copy(source, out, sends.at[len(copies)]))
        copies[-1].start()

    def either_way(first_out, second_out, q, part):
        source = pay.at[q, cuts(rows)[part] : cuts(rows)[part + 1]]
        copy = [pltpu.make_async_copy(source, out, sends.at[len(copies)]) for out in (first_out, second_out)]
        copies.append(copy[0])
        goes = lax.rem(me, 2) == 2 - q
        pl.when(goes)(copy[0].start)
        pl.when(jnp.logical_not(goes))(copy[1].start)

    def match(q):
        p = lax.rem(base + q, npatch)
        match_patch(p, q, q, slot, units, index, lambda n, r: blocks[n], taps, acc, pay, edges, digits)

    match(0)
    match(1)
    send(pay.at[0, PAD : PAD + side], own.at[0])
    match(2)
    add_halos(1, 0, 1, 2, pay, edges, digits)
    height = both.shape[0] // 2
    either_way(s_a, k_a, 1, 0)
    either_way(both.at[:height], both.at[height:], 1, 1)
    match(3)
    add_halos(2, 1, 2, 3, pay, edges, digits)
    either_way(s_a, k_a, 2, 0)
    either_way(both.at[:height], both.at[height:], 2, 1)
    send(pay.at[3, PAD : PAD + side], own.at[1])
    send(edges, edges_out)
    send(digits, digits_out)
    for copy in copies:
        copy.wait()


def make_turns(outer):
    last = outer - 1
    turns = [[(0, 0)], [(1, 0)], [(1, 1)], [(last - 1, 1)]]
    turns += [[(s, 0), (s, 1)] for s in range(2, last - 1)]
    return turns + [[(last - 1, 0)], [(last, 0)], [(last, 1)]]


def rest_kernel(
    npatch, dest_in, slot_in, weights_in, blocks_in, taps_in, orders_in, own, edges_in, digits_in, *rest
):
    turns = make_turns(npatch // 2)[1:]
    sent = {part: turn for turn, parts in enumerate(turns) for part in parts}
    number = len(turns) + npatch - 2
    outs = rest[:number]
    (
        acc, pay, blocks, taps, weights, wide, edges, digits,
        dest, slot, units, orders, count, index, place, sems, sends,
    ) = rest[number:]
    sources = (dest_in, weights_in, orders_in, slot_in, taps_in, edges_in, digits_in, blocks_in)
    targets = (dest, weights, orders, slot, taps, edges.at[:4], digits.at[:4], blocks)
    waits = begin(npatch, sources, targets, wide, units, count, index, sems)
    rows, side = pay.shape[1:]
    me = lax.axis_index("patch")
    base = base_of(npatch, me)
    waits[0].wait()

    def put(k, carry):
        place[orders[me, k]] = k - 2
        return carry

    lax.fori_loop(0, npatch, put, 0)
    for j in range(2):
        k = place[lax.rem(base + 3 * j, npatch)]
        waits.append(pltpu.make_async_copy(own.at[j], pay.at[k, PAD : PAD + side], sems.at[len(sources) + 1 + j]))
        waits[-1].start()

    def copies(k):
        result = []
        for j in range(2):
            begin, end = cuts(rows)[j : j + 2]
            if k % 2:
                out = outs[len(turns) + k - 1 + j]
            else:
                turn = sent[k // 2 + 1, j]
                out = outs[turn].at[begin:end] if len(turns[turn]) == 2 else outs[turn]
            result.append(pltpu.make_async_copy(pay.at[k, begin:end], out, sends.at[2 * k + j]))
        return result

    def send(q):
        mine = place[lax.rem(base + q, npatch)]
        add_halos(mine, lax.rem(q + npatch - 1, npatch), q, lax.rem(q + 1, npatch), pay, edges, digits)
        for k in range(npatch - 2):

            @pl.when(mine == k)
            def _():
                for copy in copies(k):
                    copy.start()

    for copy in waits[1:]:
        copy.wait()

    def match(q):
        p = lax.rem(base + q, npatch)
        match_patch(p, q, place[p], slot, units, index, lambda n, r: blocks[n], taps, acc, pay, edges, digits)

    def pair(i, carry):
        match(4 + 2 * i)
        match(5 + 2 * i)
        send(3 + 2 * i)
        send(4 + 2 * i)
        return carry

    lax.fori_loop(0, npatch // 2 - 2, pair, 0)
    send(npatch - 1)
    send(0)
    for k in range(npatch - 2):
        for copy in copies(k):
            copy.wait()


def match_blocks(dest, slot, weights, orders, blocks, taps):
    npatch, number = orders.shape[0], blocks.shape[0]
    edge = blocks.shape[-1]
    side = TH * edge
    rows = side + 2 * PAD
    hbm = pl.BlockSpec(memory_space=pltpu.HBM)
    part = [jax.ShapeDtypeStruct((end - begin, side), jnp.bfloat16) for begin, end in zip(cuts(rows), cuts(rows)[1:])]
    whole = jax.ShapeDtypeStruct((rows, side), jnp.bfloat16)
    params = pltpu.CompilerParams(vmem_limit_bytes=64 * 1024 * 1024)
    ints = pltpu.SMEM((1, number), jnp.int32)

    def scratch(payloads, patches):
        return [
            pltpu.VMEM((SLOTS, edge, edge), jnp.float32),
            pltpu.VMEM((payloads, rows, side), jnp.bfloat16),
            pltpu.VMEM(blocks.shape, jnp.bfloat16),
            pltpu.VMEM(taps.shape, jnp.bfloat16),
            pltpu.VMEM((1, number), jnp.bfloat16),
            pltpu.VMEM((1, number), jnp.int32),
            pltpu.VMEM((patches, 2, PAD, side), jnp.bfloat16),
            pltpu.VMEM((patches, 8, 128), jnp.float32),
            ints,
            ints,
            ints,
        ]

    count = pltpu.SMEM((npatch,), jnp.int32)
    index = pltpu.SMEM((npatch * CAP,), jnp.int32)
    s_a, k_a, both, own, edges, digits = pl.pallas_call(
        lambda *refs: first_kernel(npatch, *refs),
        out_shape=[part[0]] * 2
        + [
            jax.ShapeDtypeStruct((2 * part[1].shape[0], side), jnp.bfloat16),
            jax.ShapeDtypeStruct((2, side, side), jnp.bfloat16),
            jax.ShapeDtypeStruct((4, 2, PAD, side), jnp.bfloat16),
            jax.ShapeDtypeStruct((4, 8, 128), jnp.float32),
        ],
        in_specs=[hbm] * 5,
        out_specs=[hbm] * 6,
        scratch_shapes=[
            *scratch(4, 4),
            count,
            index,
            pltpu.SemaphoreType.DMA((6,)),
            pltpu.SemaphoreType.DMA((8,)),
        ],
        compiler_params=params,
        name="match_first",
    )(dest, slot, weights, blocks, taps)
    turns = make_turns(npatch // 2)
    outs = pl.pallas_call(
        lambda *refs: rest_kernel(npatch, *refs),
        out_shape=[whole if len(turn) == 2 else part[turn[0][1]] for turn in turns[1:]] + part * (npatch // 2 - 1),
        in_specs=[hbm] * 9,
        out_specs=[hbm] * (len(turns) - 1 + npatch - 2),
        scratch_shapes=[
            *scratch(npatch - 2, npatch),
            pltpu.SMEM(orders.shape, jnp.int32),
            count,
            index,
            pltpu.SMEM((npatch,), jnp.int32),
            pltpu.SemaphoreType.DMA((11,)),
            pltpu.SemaphoreType.DMA((2 * (npatch - 2),)),
        ],
        compiler_params=params,
        cost_estimate=pl.CostEstimate(flops=2_000_000_000, bytes_accessed=8_000_000, transcendentals=0),
        name="match_rest",
    )(dest, slot, weights, blocks, taps, jnp.asarray(orders), own, edges, digits)
    sends = [s_a] + list(outs[: len(turns) - 1])
    kept = outs[len(turns) - 1 :]
    return sends, [(k_a, None)] + [(kept[2 * k], kept[2 * k + 1]) for k in range(npatch // 2 - 1)], both


def split(value):
    high = value.astype(jnp.bfloat16)
    return high, (value - high.astype(jnp.float32)).astype(jnp.bfloat16)


def dot3(ah, al, bh, bl, dims):
    def one(a, b):
        return lax.dot_general(a, b, (dims, ((), ())), preferred_element_type=jnp.float32)

    return one(ah, bh) + (one(ah, bl) + one(al, bh))


def chi_rows(place, rowh, rowl, ch, cl, noise):
    rows = pl.ds(pl.multiple_of(place * 128, 128), 128)
    row_pass = dot3(rowh[rows, :], rowl[rows, :], ch, cl, ((1,), (1,)))
    return row_pass * row_pass * (1.0 / noise[0])


def total(x0, x1, x2, x3):
    f32 = jnp.float32
    return x0[...].astype(f32) + x1[...].astype(f32) + (x2[...].astype(f32) + x3[...].astype(f32))


def column_pass(colh, coll, padded):
    high, low = split(padded)
    return split(dot3(colh[...], coll[...], high, low, ((1,), (0,))))


def tail_left(a0, a1, a2, a3, noise, band, colh, coll, rowh, rowl, normed, seam, factor, give, stay):
    f32 = jnp.float32
    rows, side = a0.shape
    edge = side // TH
    left = total(a0, a1, a2, a3)
    lane = lax.broadcasted_iota(jnp.int32, (1, side), 1)
    power = lax.shift_left(jnp.ones((1, side), jnp.int32), lane % DIGITS).astype(f32) * (1.0 / UNIT)
    value = left[0:1, :] * power

    def scale(group, s):
        here = (lane >= group * 128 + s * DIGITS) & (lane < group * 128 + (s + 1) * DIGITS)
        weight_sum = jnp.sum(jnp.where(here, value, 0.0), axis=1, keepdims=True)
        return jnp.broadcast_to(1.0 / jnp.maximum(weight_sum, 1.0), (1, edge))

    def factors(group, column):
        return jnp.concatenate([scale(group, r * TW + column) for r in range(TH)], axis=1)

    right = factors(0, 1)
    left = jnp.concatenate(
        [left[:PAD] * factors(1, TW - 1), left[PAD : PAD + edge] * factors(0, 0), left[PAD + edge :] * right], axis=0
    )
    normed[...] = left[PAD : PAD + edge]
    seam[...] = left[edge:]
    factor[0] = jnp.broadcast_to(right, (8, side))
    factor[1] = jnp.broadcast_to(factors(2, 0), (8, side))
    ch, cl = column_pass(colh, coll, left)
    for j, place in enumerate((band[0], band[0] ^ 2)):
        give[j] = chi_rows(place ^ 1, rowh, rowl, ch, cl, noise)
        stay[j] = chi_rows(place, rowh, rowl, ch, cl, noise)


def tail_right(
    b0, b1, b2, b3, seam, factor, give_left, stay_left, noise, band, colh, coll, rowh, rowl, normed, give, stay
):
    rows, side = b0.shape
    edge = side // TH
    right = total(b0, b1, b2, b3)
    inner = edge - PAD
    right = jnp.concatenate([seam[...], right[:inner] * factor[0, 0:1], right[inner:] * factor[1, 0:1]], axis=0)
    normed[...] = right[PAD : PAD + edge]
    ch, cl = column_pass(colh, coll, right)
    for j, place in enumerate((band[0], band[0] ^ 2)):
        give[j, :, edge:] = chi_rows(place ^ 1, rowh, rowl, ch, cl, noise).astype(give.dtype)
        stay[j, :, edge:] = chi_rows(place, rowh, rowl, ch, cl, noise)
        give[j, :, :edge] = give_left[j].astype(give.dtype)
        stay[j, :, :edge] = stay_left[j]


def tail_image(left, right, image):
    edge = left.shape[0]
    image[:, :edge] = left[...].T
    image[:, edge:] = right[...].T


def tables_kernel(det, colh, coll, rowh, rowl):
    for high, low, start in ((colh, coll, DR - PAD), (rowh, rowl, DR)):
        offsets = (
            lax.broadcasted_iota(jnp.int32, high.shape, 1)
            - lax.broadcasted_iota(jnp.int32, high.shape, 0)
            + start
        )
        table = jnp.zeros(high.shape, jnp.float32)
        for tap in range(det.shape[1]):
            table = jnp.where(offsets == tap, det[0, tap], table)
        high[...], low[...] = split(table)


def filter_tables(det, rows, side):
    return pl.pallas_call(
        tables_kernel,
        out_shape=[jax.ShapeDtypeStruct(s, jnp.bfloat16) for s in [(side // TW, rows)] * 2 + [(side, side)] * 2],
        in_specs=[pl.BlockSpec(memory_space=pltpu.SMEM)],
        out_specs=[pl.BlockSpec(memory_space=pltpu.VMEM)] * 4,
        compiler_params=pltpu.CompilerParams(vmem_limit_bytes=40 * 1024 * 1024),
        cost_estimate=pl.CostEstimate(flops=20_000_000, bytes_accessed=2_000_000, transcendentals=0),
        name="tables",
    )(det)


def finish(left, right, noise, det):
    rows, side = left[0].shape
    f32, bf16 = jnp.float32, jnp.bfloat16
    colh, coll, rowh, rowl = filter_tables(det, rows, side)
    band = lax.axis_index("band")
    where = band.reshape(1).astype(jnp.int32)
    smem = pl.BlockSpec(memory_space=pltpu.SMEM)
    vmem = pl.BlockSpec(memory_space=pltpu.VMEM)
    params = pltpu.CompilerParams(vmem_limit_bytes=40 * 1024 * 1024)
    quarters = jax.ShapeDtypeStruct((2, side // 4, side // TW), f32)
    tile = jax.ShapeDtypeStruct((side // TW, side), f32)
    tables = (colh, coll, rowh, rowl)

    normed_left, seam, factor, give, stay = pl.pallas_call(
        tail_left,
        out_shape=[
            tile,
            jax.ShapeDtypeStruct((2 * PAD, side), f32),
            jax.ShapeDtypeStruct((2, 8, side), f32),
            quarters,
            quarters,
        ],
        in_specs=[vmem] * 4 + [smem] * 2 + [vmem] * 4,
        out_specs=[vmem] * 5,
        compiler_params=params,
        cost_estimate=pl.CostEstimate(flops=500_000_000, bytes_accessed=4_000_000, transcendentals=0),
        name="tail_left",
    )(*left, noise, where, *tables)
    normed_right, give, stay = pl.pallas_call(
        tail_right,
        out_shape=[
            tile,
            jax.ShapeDtypeStruct((2, side // 4, side), bf16),
            jax.ShapeDtypeStruct((2, side // 4, side), f32),
        ],
        in_specs=[vmem] * 8 + [smem] * 2 + [vmem] * 4,
        out_specs=[vmem] * 3,
        compiler_params=params,
        name="tail_right",
    )(*right, seam, factor, give, stay, noise, where, *tables)
    pair = stay + lax.ppermute(give, "band", [(i, i ^ 1) for i in range(4)]).astype(f32)
    beyond = lax.ppermute(pair[1].astype(bf16), "band", [(i, i ^ 2) for i in range(4)])
    normed_right, _ = lax.optimization_barrier((normed_right, pair))
    image = pl.pallas_call(
        tail_image,
        out_shape=jax.ShapeDtypeStruct((side, side), f32),
        in_specs=[vmem] * 2,
        out_specs=vmem,
        compiler_params=params,
        cost_estimate=pl.CostEstimate(flops=0, bytes_accessed=2_000_000, transcendentals=0),
        name="tail_image",
    )(normed_left, normed_right)
    return image, pair[0] + beyond.astype(f32)


def either(flags):
    result = flags[0]
    for flag in flags[1:]:
        result = result | flag
    return result


def local(blocks, dest_patch, dest_slot, weights, psf_taps, det_taps, noise_var):
    f32, bf16 = jnp.float32, jnp.bfloat16
    npatch = lax.axis_size("patch")
    outer = npatch // 2
    me = lax.axis_index("patch")
    z = me // 2
    table = dest_table(outer)
    where_is = np.argsort(table, axis=1)
    order = np.zeros((npatch, npatch), np.int32)
    for i in range(npatch):
        for s in range(outer):
            order[i, 2 * s] = table[i // 2, s] * 2 + 1 - i % 2
            order[i, 2 * s + 1] = table[i // 2, s] * 2 + i % 2
    sends, kept, both = match_blocks(dest_patch, dest_slot, weights, order, blocks[0], psf_taps[0])
    last = outer - 1
    nband = lax.axis_size("band")
    across = [(i, i ^ 1) for i in range(npatch)]
    even = [(i, i ^ 2) for i in range(npatch)]
    odd = []
    for i in range(npatch):
        q = i // 2
        to = q + 1 if q % 2 else q - 1
        for j in range(nband):
            if 0 <= to < outer:
                odd.append((i * nband + j, (2 * to + i % 2) * nband + j))
            else:
                odd.append((i * nband + j, i * nband + (j ^ 1)))
    ends, beside_ends = (0, last), (1, last - 1)

    def place_in(places):
        return either([z == q for q in places])

    def only(places, value):
        return jnp.where(place_in(places), value.astype(f32), 0.0)

    half = both.shape[0] // 2
    with jax.named_scope("even_step_0_right"):
        direct = lax.ppermute(both, "patch", even)
    came = {}
    got = []

    def across_y(send):
        i = len(got)
        if i in (1, 2):
            send, _ = lax.optimization_barrier((send, got[0]))
        if i > 3:
            send, _, _ = lax.optimization_barrier((send, got[i - 2], got[i - 3]))
        with jax.named_scope(f"across_turn_{i}_of"):
            got.append(lax.ppermute(send, "patch", across))

    turns = make_turns(outer)
    for parts, send in zip(turns[:-1], sends, strict=False):
        if len(got) == 3:
            paired = both[:half].astype(f32) + only(beside_ends, direct[:half])
            send = jnp.where(place_in(ends), send.astype(f32), paired).astype(bf16)
        across_y(send)
        for part in parts:
            begin, end = cuts(got[-1].shape[0])[part[1] :][:2]
            came[part] = got[-1][begin:end] if len(parts) == 2 else got[-1]

    def combined(s, c):
        if (s, c) == (0, 1):
            mine = both[half:].astype(f32) + only(beside_ends, direct[half:])
            return mine + came[last - 1, 1].astype(f32)
        if (s, c) == (last - 1, 1):
            return kept[s][c].astype(f32) + only(ends, came[s, c])
        mine, other = kept[s][c], came[s, c]
        if s == 0:
            other, _ = lax.optimization_barrier((other, sends[1]))
        return mine.astype(f32) + other.astype(f32)

    def chosen(places, c):
        values = sorted(set(places.values()))
        result = combined(values[-1], c)
        for v in values[:-1]:
            result = jnp.where(either([z == q for q, s in places.items() if s == v]), combined(v, c), result)
        return result

    def step(t, parity, c):
        places = {}
        for q in range(outer):
            rising = q % 2 == parity
            hops = q if rising else last - q
            d = last - t + q if rising else t - hops
            if hops <= t and 0 <= d < outer and d != q:
                places[q] = int(where_is[q][d])
        return chosen(places, c)

    def masked(value):
        return jnp.where(place_in(ends), 0.0, value.astype(f32))

    evens, odds, send_even = [None, None], [None, None], [None, None]
    for t in range(last):
        for c in range(2):
            side = "left" if c == 0 else "right"
            if (t, c) == (1, 1):
                came[1, 1], *_ = lax.optimization_barrier((came[1, 1], *earlier))
            send = None if (t, c) == (0, 1) else step(t, 0, c)
            if (t, c) == (2, 0):
                odds[0], _ = lax.optimization_barrier((odds[0], sent_odd))
            if t > 1:
                send = send + masked(odds[c])
            if (t, c) == (1, 1):
                ahead = (step(2, 1, 0) + evens[0].astype(f32)).astype(bf16)
            send_odd = step(t, 1, c) if t else None
            if (t, c) == (2, 1):
                send, _ = lax.optimization_barrier((send, came[last, 0]))
            if (t, c) == (2, 0):
                send_odd = ahead
            elif t and (t, c) != (1, 1):
                send_odd = send_odd + evens[c].astype(f32)
            if (t, c) == (1, 1):
                passing, _ = lax.optimization_barrier((sends[3], got[1]))
                send = jnp.where(place_in(ends), send, passing.astype(f32))
            if send is not None:
                with jax.named_scope(f"even_step_{t}_{side}"):
                    send_even[c] = send.astype(bf16)
                    evens[c] = lax.ppermute(send_even[c], "patch", even)
            if (t, c) == (1, 1):
                evens[c], *_ = lax.optimization_barrier((evens[c], ahead, odds[0]))
                passed = jnp.where(place_in(beside_ends), 0.0, evens[c].astype(f32))
                final = (sends[-1].astype(f32) + passed).astype(bf16)
            if (t, c) == (1, 1):
                det_taps, _ = lax.optimization_barrier((det_taps, evens[c]))
            if (t, c) == (2, 1):
                send_odd, _ = lax.optimization_barrier((send_odd.astype(bf16), send_even[0]))
            if (t, c) == (1, 0):
                earlier = send_even[0], send_odd.astype(bf16)
            if t:
                sent_odd = send_odd.astype(bf16)
                with jax.named_scope(f"odd_step_{t}_{side}"):
                    odds[c] = lax.ppermute(send_odd.astype(bf16), ("patch", "band"), odd)
            if (t, c) == (2, 1):
                final, _ = lax.optimization_barrier((final, send_even[1]))
                across_y(final)
                came[last, 1] = got[-1]
    odds[1], _ = lax.optimization_barrier((odds[1], evens[0]))
    for c in range(2):
        odds[c] = masked(odds[c]).astype(bf16)
    parts = [(kept[last][c], came[last, c], evens[c], odds[c]) for c in range(2)]
    image, chi = finish(*parts, noise_var, det_taps)
    return image[None], chi


def solution(mesh):
    in_specs = (
        P("band", "patch", None, None),
        P("band", "patch"),
        P("band", "patch"),
        P("band", "patch"),
        P("band", "patch", None, None),
        P("band", None),
        P("band"),
    )
    out_specs = (P("band", None, "patch"), P("band", "patch"))
    return jax.shard_map(local, mesh=mesh, in_specs=in_specs, out_specs=out_specs, check_vma=False)
```

```python
import jax
import jax.numpy as jnp
import numpy as np
from jax import lax
from jax.experimental import pallas as pl
from jax.experimental.pallas import tpu as pltpu
from jax.sharding import PartitionSpec as P

TH = 2
TW = 2
DR = 12
CAP = 4
SLOTS = 4
PAD = 16
DIGITS = 16
UNIT = 512


def cuts(rows):
    return (0, rows // 2 + PAD, rows)


def dest_table(outer):
    table = np.zeros((outer, outer), np.int32)
    for z in range(outer):
        def due(d):
            if d > z:
                return (outer - 1 + z - d, d == z ^ 1)
            if d < z:
                return (outer - 1 - z + d, d == z ^ 1)
            return (outer, 0)

        table[z] = sorted(range(outer), key=due)
    return table


def toeplitz(row):
    half = row.shape[1] // 2
    wide = jnp.broadcast_to(row, (half, 2 * half))
    skew = pltpu.roll(wide, 0, 1, stride=1, stride_axis=0)
    diag = skew[:, :half]
    off = skew[:, half:]
    i = lax.broadcasted_iota(jnp.int32, (half, half), 0)
    j = lax.broadcasted_iota(jnp.int32, (half, half), 1)
    upper = jnp.where(j < i, off, 0.0)
    lower = jnp.where(j > i, off, 0.0)
    top = jnp.concatenate([diag, upper], axis=1)
    bottom = jnp.concatenate([lower, diag], axis=1)
    return jnp.concatenate([top, bottom], axis=0).astype(jnp.bfloat16)


def make_lists(npatch, dest, count, index):
    def clear(p, carry):
        count[p] = 0
        for r in range(CAP):
            index[p * CAP + r] = -1
        return carry

    lax.fori_loop(0, npatch, clear, 0)

    def place(n, carry):
        p = dest[0, n]
        r = count[p]
        count[p] = r + 1
        index[p * CAP + r] = n
        return carry

    lax.fori_loop(0, dest.shape[1], place, 0)


def match_patch(p, q, k, slot, units, index, block, taps, acc, pay, edges, digits):
    edge = acc.shape[-1]
    ntaps = taps.shape[-1]
    side = TH * edge
    lane = lax.broadcasted_iota(jnp.int32, (8, 128), 1)
    acc[...] = jnp.zeros(acc.shape, acc.dtype)
    row = jnp.zeros((8, 128), jnp.float32)
    for r in range(CAP):
        found = index[p * CAP + r]
        n = jnp.maximum(found, 0)
        s = slot[0, n]
        unit = jnp.where(found >= 0, units[0, n], 0)
        w = unit.astype(jnp.float32) * (1.0 / UNIT)
        tap = taps[n].astype(jnp.float32)
        tap = jnp.concatenate([tap, jnp.zeros((2, edge - ntaps), jnp.float32)], axis=1)
        tap = pltpu.roll(tap, edge - ntaps // 2, 1)
        col = toeplitz(tap[0:1])
        half = jnp.dot(col, block(n, r), preferred_element_type=jnp.float32).astype(jnp.bfloat16)
        rowm = toeplitz(tap[1:2])
        matched = lax.dot_general(
            rowm, half, (((1,), (1,)), ((), ())), preferred_element_type=jnp.float32
        ).astype(jnp.bfloat16)
        acc[s] = acc[s] + w * matched.astype(jnp.float32)
        bit = lax.shift_right_logical(jnp.full((8, 128), unit), lane % DIGITS) & 1
        row = row + jnp.where(lane // DIGITS == s, bit, 0).astype(jnp.float32)
    digits[q] = row
    for s in range(SLOTS):
        top = (s % TW) * edge
        left = (s // TW) * edge
        pay[k, PAD + top : PAD + top + edge, left : left + edge] = acc[s].astype(jnp.bfloat16)
    edges[q, 0] = pay[k, PAD : 2 * PAD, :]
    edges[q, 1] = pay[k, side : side + PAD, :]


def add_halos(k, before, q, after, pay, edges, digits):
    rows, side = pay.shape[1:]
    first = lax.broadcasted_iota(jnp.int32, (PAD, side), 0) == 0
    blank = jnp.zeros((8, side - 3 * 128), jnp.float32)
    row = jnp.concatenate([digits[q], digits[before], digits[after], blank], axis=1)
    row = jnp.concatenate([row, row], axis=0)
    pay[k, :PAD, :] = jnp.where(first, row, edges[before, 1].astype(jnp.float32)).astype(jnp.bfloat16)
    pay[k, rows - PAD :, :] = edges[after, 0]


def begin(npatch, sources, targets, wide, units, count, index, sems):
    fetched = [pltpu.make_async_copy(x, y, sems.at[i]) for i, (x, y) in enumerate(zip(sources, targets, strict=True))]
    for copy in fetched:
        copy.start()
    dest, weights = targets[:2]
    fetched[1].wait()
    wide[...] = (weights[...].astype(jnp.float32) * UNIT).astype(jnp.int32)
    convert = pltpu.make_async_copy(wide, units, sems.at[len(fetched)])
    convert.start()
    fetched[0].wait()
    make_lists(npatch, dest, count, index)
    return [*fetched[2:], convert]


def base_of(npatch, me):
    return jnp.where(2 * (me // 2) < npatch // 2, npatch - 3, npatch - 1)


def first_kernel(
    npatch, dest_in, slot_in, weights_in, blocks_in, taps_in, s_a, k_a, both, own, edges_out, digits_out,
    acc, pay, blocks, taps, weights, wide, edges, digits, dest, slot, units, count, index, sems, sends,
):
    sources = (dest_in, weights_in, slot_in, taps_in, blocks_in)
    waits = begin(npatch, sources, (dest, weights, slot, taps, blocks), wide, units, count, index, sems)
    me = lax.axis_index("patch")
    base = base_of(npatch, me)
    for copy in waits:
        copy.wait()
    rows, side = pay.shape[1:]
    copies = []

    def send(source, out):
        copies.append(pltpu.make_async_copy(source, out, sends.at[len(copies)]))
        copies[-1].start()

    def either_way(first_out, second_out, q, part):
        source = pay.at[q, cuts(rows)[part] : cuts(rows)[part + 1]]
        copy = [pltpu.make_async_copy(source, out, sends.at[len(copies)]) for out in (first_out, second_out)]
        copies.append(copy[0])
        goes = lax.rem(me, 2) == 2 - q
        pl.when(goes)(copy[0].start)
        pl.when(jnp.logical_not(goes))(copy[1].start)

    def match(q):
        p = lax.rem(base + q, npatch)
        match_patch(p, q, q, slot, units, index, lambda n, r: blocks[n], taps, acc, pay, edges, digits)

    match(0)
    match(1)
    send(pay.at[0, PAD : PAD + side], own.at[0])
    match(2)
    add_halos(1, 0, 1, 2, pay, edges, digits)
    height = both.shape[0] // 2
    either_way(s_a, k_a, 1, 0)
    either_way(both.at[:height], both.at[height:], 1, 1)
    match(3)
    add_halos(2, 1, 2, 3, pay, edges, digits)
    either_way(s_a, k_a, 2, 0)
    either_way(both.at[:height], both.at[height:], 2, 1)
    send(pay.at[3, PAD : PAD + side], own.at[1])
    send(edges, edges_out)
    send(digits, digits_out)
    for copy in copies:
        copy.wait()


def make_turns(outer):
    last = outer - 1
    turns = [[(0, 0)], [(1, 0)], [(1, 1)], [(last - 1, 1)]]
    turns += [[(s, 0), (s, 1)] for s in range(2, last - 1)]
    return turns + [[(last - 1, 0)], [(last, 0)], [(last, 1)]]


def rest_kernel(
    npatch, dest_in, slot_in, weights_in, blocks_in, taps_in, orders_in, own, edges_in, digits_in, *rest
):
    turns = make_turns(npatch // 2)[1:]
    sent = {part: turn for turn, parts in enumerate(turns) for part in parts}
    number = len(turns) + npatch - 2
    outs = rest[:number]
    (
        acc, pay, blocks, taps, weights, wide, edges, digits,
        dest, slot, units, orders, count, index, place, sems, sends,
    ) = rest[number:]
    sources = (dest_in, weights_in, orders_in, slot_in, taps_in, edges_in, digits_in, blocks_in)
    targets = (dest, weights, orders, slot, taps, edges.at[:4], digits.at[:4], blocks)
    waits = begin(npatch, sources, targets, wide, units, count, index, sems)
    rows, side = pay.shape[1:]
    me = lax.axis_index("patch")
    base = base_of(npatch, me)
    waits[0].wait()

    def put(k, carry):
        place[orders[me, k]] = k - 2
        return carry

    lax.fori_loop(0, npatch, put, 0)
    for j in range(2):
        k = place[lax.rem(base + 3 * j, npatch)]
        waits.append(pltpu.make_async_copy(own.at[j], pay.at[k, PAD : PAD + side], sems.at[len(sources) + 1 + j]))
        waits[-1].start()

    def copies(k):
        result = []
        for j in range(2):
            begin, end = cuts(rows)[j : j + 2]
            if k % 2:
                out = outs[len(turns) + k - 1 + j]
            else:
                turn = sent[k // 2 + 1, j]
                out = outs[turn].at[begin:end] if len(turns[turn]) == 2 else outs[turn]
            result.append(pltpu.make_async_copy(pay.at[k, begin:end], out, sends.at[2 * k + j]))
        return result

    def send(q):
        mine = place[lax.rem(base + q, npatch)]
        add_halos(mine, lax.rem(q + npatch - 1, npatch), q, lax.rem(q + 1, npatch), pay, edges, digits)
        for k in range(npatch - 2):

            @pl.when(mine == k)
            def _():
                for copy in copies(k):
                    copy.start()

    for copy in waits[1:]:
        copy.wait()

    def match(q):
        p = lax.rem(base + q, npatch)
        match_patch(p, q, place[p], slot, units, index, lambda n, r: blocks[n], taps, acc, pay, edges, digits)

    def pair(i, carry):
        match(4 + 2 * i)
        match(5 + 2 * i)
        send(3 + 2 * i)
        send(4 + 2 * i)
        return carry

    lax.fori_loop(0, npatch // 2 - 2, pair, 0)
    send(npatch - 1)
    send(0)
    for k in range(npatch - 2):
        for copy in copies(k):
            copy.wait()


def match_blocks(dest, slot, weights, orders, blocks, taps):
    npatch, number = orders.shape[0], blocks.shape[0]
    edge = blocks.shape[-1]
    side = TH * edge
    rows = side + 2 * PAD
    hbm = pl.BlockSpec(memory_space=pltpu.HBM)
    part = [jax.ShapeDtypeStruct((end - begin, side), jnp.bfloat16) for begin, end in zip(cuts(rows), cuts(rows)[1:])]
    whole = jax.ShapeDtypeStruct((rows, side), jnp.bfloat16)
    params = pltpu.CompilerParams(vmem_limit_bytes=64 * 1024 * 1024)
    ints = pltpu.SMEM((1, number), jnp.int32)

    def scratch(payloads, patches):
        return [
            pltpu.VMEM((SLOTS, edge, edge), jnp.float32),
            pltpu.VMEM((payloads, rows, side), jnp.bfloat16),
            pltpu.VMEM(blocks.shape, jnp.bfloat16),
            pltpu.VMEM(taps.shape, jnp.bfloat16),
            pltpu.VMEM((1, number), jnp.bfloat16),
            pltpu.VMEM((1, number), jnp.int32),
            pltpu.VMEM((patches, 2, PAD, side), jnp.bfloat16),
            pltpu.VMEM((patches, 8, 128), jnp.float32),
            ints,
            ints,
            ints,
        ]

    count = pltpu.SMEM((npatch,), jnp.int32)
    index = pltpu.SMEM((npatch * CAP,), jnp.int32)
    s_a, k_a, both, own, edges, digits = pl.pallas_call(
        lambda *refs: first_kernel(npatch, *refs),
        out_shape=[part[0]] * 2
        + [
            jax.ShapeDtypeStruct((2 * part[1].shape[0], side), jnp.bfloat16),
            jax.ShapeDtypeStruct((2, side, side), jnp.bfloat16),
            jax.ShapeDtypeStruct((4, 2, PAD, side), jnp.bfloat16),
            jax.ShapeDtypeStruct((4, 8, 128), jnp.float32),
        ],
        in_specs=[hbm] * 5,
        out_specs=[hbm] * 6,
        scratch_shapes=[
            *scratch(4, 4),
            count,
            index,
            pltpu.SemaphoreType.DMA((6,)),
            pltpu.SemaphoreType.DMA((8,)),
        ],
        compiler_params=params,
        name="match_first",
    )(dest, slot, weights, blocks, taps)
    turns = make_turns(npatch // 2)
    outs = pl.pallas_call(
        lambda *refs: rest_kernel(npatch, *refs),
        out_shape=[whole if len(turn) == 2 else part[turn[0][1]] for turn in turns[1:]] + part * (npatch // 2 - 1),
        in_specs=[hbm] * 9,
        out_specs=[hbm] * (len(turns) - 1 + npatch - 2),
        scratch_shapes=[
            *scratch(npatch - 2, npatch),
            pltpu.SMEM(orders.shape, jnp.int32),
            count,
            index,
            pltpu.SMEM((npatch,), jnp.int32),
            pltpu.SemaphoreType.DMA((11,)),
            pltpu.SemaphoreType.DMA((2 * (npatch - 2),)),
        ],
        compiler_params=params,
        cost_estimate=pl.CostEstimate(flops=2_000_000_000, bytes_accessed=8_000_000, transcendentals=0),
        name="match_rest",
    )(dest, slot, weights, blocks, taps, jnp.asarray(orders), own, edges, digits)
    sends = [s_a] + list(outs[: len(turns) - 1])
    kept = outs[len(turns) - 1 :]
    return sends, [(k_a, None)] + [(kept[2 * k], kept[2 * k + 1]) for k in range(npatch // 2 - 1)], both


def split(value):
    high = value.astype(jnp.bfloat16)
    return high, (value - high.astype(jnp.float32)).astype(jnp.bfloat16)


def dot3(ah, al, bh, bl, dims):
    def one(a, b):
        return lax.dot_general(a, b, (dims, ((), ())), preferred_element_type=jnp.float32)

    return one(ah, bh) + (one(ah, bl) + one(al, bh))


def chi_rows(place, rowh, rowl, ch, cl, noise):
    rows = pl.ds(pl.multiple_of(place * 128, 128), 128)
    row_pass = dot3(rowh[rows, :], rowl[rows, :], ch, cl, ((1,), (1,)))
    return row_pass * row_pass * (1.0 / noise[0])


def total(x0, x1, x2, x3):
    f32 = jnp.float32
    return x0[...].astype(f32) + x1[...].astype(f32) + (x2[...].astype(f32) + x3[...].astype(f32))


def column_pass(colh, coll, padded):
    high, low = split(padded)
    return split(dot3(colh[...], coll[...], high, low, ((1,), (0,))))


def tail_left(a0, a1, a2, a3, noise, band, colh, coll, rowh, rowl, normed, seam, factor, give, stay):
    f32 = jnp.float32
    rows, side = a0.shape
    edge = side // TH
    left = total(a0, a1, a2, a3)
    lane = lax.broadcasted_iota(jnp.int32, (1, side), 1)
    power = lax.shift_left(jnp.ones((1, side), jnp.int32), lane % DIGITS).astype(f32) * (1.0 / UNIT)
    value = left[0:1, :] * power

    def scale(group, s):
        here = (lane >= group * 128 + s * DIGITS) & (lane < group * 128 + (s + 1) * DIGITS)
        weight_sum = jnp.sum(jnp.where(here, value, 0.0), axis=1, keepdims=True)
        return jnp.broadcast_to(1.0 / jnp.maximum(weight_sum, 1.0), (1, edge))

    def factors(group, column):
        return jnp.concatenate([scale(group, r * TW + column) for r in range(TH)], axis=1)

    right = factors(0, 1)
    left = jnp.concatenate(
        [left[:PAD] * factors(1, TW - 1), left[PAD : PAD + edge] * factors(0, 0), left[PAD + edge :] * right], axis=0
    )
    normed[...] = left[PAD : PAD + edge]
    seam[...] = left[edge:]
    factor[0] = jnp.broadcast_to(right, (8, side))
    factor[1] = jnp.broadcast_to(factors(2, 0), (8, side))
    ch, cl = column_pass(colh, coll, left)
    for j, place in enumerate((band[0], band[0] ^ 2)):
        give[j] = chi_rows(place ^ 1, rowh, rowl, ch, cl, noise)
        stay[j] = chi_rows(place, rowh, rowl, ch, cl, noise)


def tail_right(
    b0, b1, b2, b3, seam, factor, give_left, stay_left, noise, band, colh, coll, rowh, rowl, normed, give_near, give_far, stay
):
    rows, side = b0.shape
    edge = side // TH
    right = total(b0, b1, b2, b3)
    inner = edge - PAD
    right = jnp.concatenate([seam[...], right[:inner] * factor[0, 0:1], right[inner:] * factor[1, 0:1]], axis=0)
    normed[...] = right[PAD : PAD + edge]
    ch, cl = column_pass(colh, coll, right)
    for j, (place, give) in enumerate(((band[0], give_near), (band[0] ^ 2, give_far))):
        give[:, edge:] = chi_rows(place ^ 1, rowh, rowl, ch, cl, noise).astype(give.dtype)
        stay[j, :, edge:] = chi_rows(place, rowh, rowl, ch, cl, noise)
        give[:, :edge] = give_left[j].astype(give.dtype)
        stay[j, :, :edge] = stay_left[j]


def tail_image(left, right, image):
    edge = left.shape[0]
    image[:, :edge] = left[...].T
    image[:, edge:] = right[...].T


def tables_kernel(det, colh, coll, rowh, rowl):
    for high, low, start in ((colh, coll, DR - PAD), (rowh, rowl, DR)):
        offsets = (
            lax.broadcasted_iota(jnp.int32, high.shape, 1)
            - lax.broadcasted_iota(jnp.int32, high.shape, 0)
            + start
        )
        table = jnp.zeros(high.shape, jnp.float32)
        for tap in range(det.shape[1]):
            table = jnp.where(offsets == tap, det[0, tap], table)
        high[...], low[...] = split(table)


def filter_tables(det, rows, side):
    return pl.pallas_call(
        tables_kernel,
        out_shape=[jax.ShapeDtypeStruct(s, jnp.bfloat16) for s in [(side // TW, rows)] * 2 + [(side, side)] * 2],
        in_specs=[pl.BlockSpec(memory_space=pltpu.SMEM)],
        out_specs=[pl.BlockSpec(memory_space=pltpu.VMEM)] * 4,
        compiler_params=pltpu.CompilerParams(vmem_limit_bytes=40 * 1024 * 1024),
        cost_estimate=pl.CostEstimate(flops=20_000_000, bytes_accessed=2_000_000, transcendentals=0),
        name="tables",
    )(det)


def finish(left, right, masked, noise, det):
    rows, side = left[0].shape
    f32, bf16 = jnp.float32, jnp.bfloat16
    colh, coll, rowh, rowl = filter_tables(det, rows, side)
    band = lax.axis_index("band")
    where = band.reshape(1).astype(jnp.int32)
    smem = pl.BlockSpec(memory_space=pltpu.SMEM)
    vmem = pl.BlockSpec(memory_space=pltpu.VMEM)
    params = pltpu.CompilerParams(vmem_limit_bytes=40 * 1024 * 1024)
    quarters = jax.ShapeDtypeStruct((2, side // 4, side // TW), f32)
    tile = jax.ShapeDtypeStruct((side // TW, side), f32)
    tables = (colh, coll, rowh, rowl)

    normed_left, seam, factor, give, stay = pl.pallas_call(
        tail_left,
        out_shape=[
            tile,
            jax.ShapeDtypeStruct((2 * PAD, side), f32),
            jax.ShapeDtypeStruct((2, 8, side), f32),
            quarters,
            quarters,
        ],
        in_specs=[vmem] * 4 + [smem] * 2 + [vmem] * 4,
        out_specs=[vmem] * 5,
        compiler_params=params,
        cost_estimate=pl.CostEstimate(flops=500_000_000, bytes_accessed=4_000_000, transcendentals=0),
        name="tail_left",
    )(*left, noise, where, *tables)
    *right, odd_right = right
    odd_right, _ = lax.optimization_barrier((odd_right, seam))
    right = [*right, masked(odd_right).astype(bf16)]
    quarter = jax.ShapeDtypeStruct((side // 4, side), bf16)
    normed_right, give_near, give_far, stay = pl.pallas_call(
        tail_right,
        out_shape=[tile, quarter, quarter, jax.ShapeDtypeStruct((2, side // 4, side), f32)],
        in_specs=[vmem] * 8 + [smem] * 2 + [vmem] * 4,
        out_specs=[vmem] * 4,
        compiler_params=params,
        name="tail_right",
    )(*right, seam, factor, give, stay, noise, where, *tables)
    core, across_x = [(i, i ^ 1) for i in range(4)], [(i, i ^ 2) for i in range(4)]
    far = (stay[1] + lax.ppermute(give_far, "band", core).astype(f32)).astype(bf16)
    beyond = lax.ppermute(far, "band", across_x)
    normed_right, give_near, _ = lax.optimization_barrier((normed_right, give_near, far))
    near = stay[0] + lax.ppermute(give_near, "band", core).astype(f32)
    image = pl.pallas_call(
        tail_image,
        out_shape=jax.ShapeDtypeStruct((side, side), f32),
        in_specs=[vmem] * 2,
        out_specs=vmem,
        compiler_params=params,
        cost_estimate=pl.CostEstimate(flops=0, bytes_accessed=2_000_000, transcendentals=0),
        name="tail_image",
    )(normed_left, normed_right)
    return image, near + beyond.astype(f32)


def either(flags):
    result = flags[0]
    for flag in flags[1:]:
        result = result | flag
    return result


def local(blocks, dest_patch, dest_slot, weights, psf_taps, det_taps, noise_var):
    f32, bf16 = jnp.float32, jnp.bfloat16
    npatch = lax.axis_size("patch")
    outer = npatch // 2
    me = lax.axis_index("patch")
    z = me // 2
    table = dest_table(outer)
    where_is = np.argsort(table, axis=1)
    order = np.zeros((npatch, npatch), np.int32)
    for i in range(npatch):
        for s in range(outer):
            order[i, 2 * s] = table[i // 2, s] * 2 + 1 - i % 2
            order[i, 2 * s + 1] = table[i // 2, s] * 2 + i % 2
    sends, kept, both = match_blocks(dest_patch, dest_slot, weights, order, blocks[0], psf_taps[0])
    last = outer - 1
    nband = lax.axis_size("band")
    across = [(i, i ^ 1) for i in range(npatch)]
    even = [(i, i ^ 2) for i in range(npatch)]
    odd = []
    for i in range(npatch):
        q = i // 2
        to = q + 1 if q % 2 else q - 1
        for j in range(nband):
            if 0 <= to < outer:
                odd.append((i * nband + j, (2 * to + i % 2) * nband + j))
            else:
                odd.append((i * nband + j, i * nband + (j ^ 1)))
    ends, beside_ends = (0, last), (1, last - 1)

    def place_in(places):
        return either([z == q for q in places])

    def only(places, value):
        return jnp.where(place_in(places), value.astype(f32), 0.0)

    half = both.shape[0] // 2
    with jax.named_scope("even_step_0_right"):
        direct = lax.ppermute(both, "patch", even)
    came = {}
    got = []

    def across_y(send):
        i = len(got)
        if i in (1, 2):
            send, _ = lax.optimization_barrier((send, got[0]))
        if i > 3:
            send, _, _ = lax.optimization_barrier((send, got[i - 2], got[i - 3]))
        with jax.named_scope(f"across_turn_{i}_of"):
            got.append(lax.ppermute(send, "patch", across))

    turns = make_turns(outer)
    for parts, send in zip(turns[:-1], sends, strict=False):
        if len(got) == 3:
            paired = both[:half].astype(f32) + only(beside_ends, direct[:half])
            send = jnp.where(place_in(ends), send.astype(f32), paired).astype(bf16)
        across_y(send)
        for part in parts:
            begin, end = cuts(got[-1].shape[0])[part[1] :][:2]
            came[part] = got[-1][begin:end] if len(parts) == 2 else got[-1]

    def combined(s, c):
        if (s, c) == (0, 1):
            mine = both[half:].astype(f32) + only(beside_ends, direct[half:])
            return mine + came[last - 1, 1].astype(f32)
        if (s, c) == (last - 1, 1):
            return kept[s][c].astype(f32) + only(ends, came[s, c])
        mine, other = kept[s][c], came[s, c]
        if s == 0:
            other, _ = lax.optimization_barrier((other, sends[1]))
        return mine.astype(f32) + other.astype(f32)

    def chosen(places, c):
        values = sorted(set(places.values()))
        result = combined(values[-1], c)
        for v in values[:-1]:
            result = jnp.where(either([z == q for q, s in places.items() if s == v]), combined(v, c), result)
        return result

    def step(t, parity, c):
        places = {}
        for q in range(outer):
            rising = q % 2 == parity
            hops = q if rising else last - q
            d = last - t + q if rising else t - hops
            if hops <= t and 0 <= d < outer and d != q:
                places[q] = int(where_is[q][d])
        return chosen(places, c)

    def masked(value):
        return jnp.where(place_in(ends), 0.0, value.astype(f32))

    evens, odds, send_even = [None, None], [None, None], [None, None]
    for t in range(last):
        for c in range(2):
            side = "left" if c == 0 else "right"
            if (t, c) == (1, 1):
                came[1, 1], *_ = lax.optimization_barrier((came[1, 1], *earlier))
            send = None if (t, c) == (0, 1) else step(t, 0, c)
            if (t, c) == (2, 0):
                odds[0], _ = lax.optimization_barrier((odds[0], sent_odd))
            if t > 1:
                send = send + masked(odds[c])
            if (t, c) == (1, 1):
                ahead = (step(2, 1, 0) + evens[0].astype(f32)).astype(bf16)
            send_odd = step(t, 1, c) if t else None
            if (t, c) == (2, 1):
                send, _ = lax.optimization_barrier((send, came[last, 0]))
            if (t, c) == (2, 0):
                send_odd = ahead
            elif t and (t, c) != (1, 1):
                send_odd = send_odd + evens[c].astype(f32)
            if (t, c) == (1, 1):
                passing, _ = lax.optimization_barrier((sends[3], got[1]))
                send = jnp.where(place_in(ends), send, passing.astype(f32))
            if send is not None:
                with jax.named_scope(f"even_step_{t}_{side}"):
                    send_even[c] = send.astype(bf16)
                    evens[c] = lax.ppermute(send_even[c], "patch", even)
            if (t, c) == (1, 1):
                evens[c], *_ = lax.optimization_barrier((evens[c], ahead, odds[0]))
                passed = jnp.where(place_in(beside_ends), 0.0, evens[c].astype(f32))
                final = (sends[-1].astype(f32) + passed).astype(bf16)
            if (t, c) == (1, 1):
                det_taps, _ = lax.optimization_barrier((det_taps, evens[c]))
            if (t, c) == (2, 1):
                send_odd, _ = lax.optimization_barrier((send_odd.astype(bf16), send_even[0]))
            if (t, c) == (1, 0):
                earlier = send_even[0], send_odd.astype(bf16)
            if t:
                sent_odd = send_odd.astype(bf16)
                with jax.named_scope(f"odd_step_{t}_{side}"):
                    odds[c] = lax.ppermute(send_odd.astype(bf16), ("patch", "band"), odd)
            if (t, c) == (2, 1):
                final, _ = lax.optimization_barrier((final, send_even[1]))
                across_y(final)
                came[last, 1] = got[-1]
    odds[0] = masked(odds[0]).astype(bf16)
    parts = [(kept[last][c], came[last, c], evens[c], odds[c]) for c in range(2)]
    image, chi = finish(*parts, masked, noise_var, det_taps)
    return image[None], chi


def solution(mesh):
    in_specs = (
        P("band", "patch", None, None),
        P("band", "patch"),
        P("band", "patch"),
        P("band", "patch"),
        P("band", "patch", None, None),
        P("band", None),
        P("band"),
    )
    out_specs = (P("band", None, "patch"), P("band", "patch"))
    return jax.shard_map(local, mesh=mesh, in_specs=in_specs, out_specs=out_specs, check_vma=False)
```
